512 devices in a mesh: rows: 16 (over z_hi, x, core), labels: 32 (over y, z_lo).
Axes of the slice: x: 4, y: 4, z: 16 (z_hi: 2, z_lo: 8; z = z_hi * 8 + z_lo), core: 2. Of those that a mesh axis runs over, the one named last changes fastest.
Arguments:
- pool_features: bfloat16 [2048, 768], P('rows'), may hold values from -6 to 6
- pool_labels: int32 [2048, 16], P('rows'), may hold values from 0 to 196607
- pool_counts: int32 [2048], P('rows'), may hold values from 1 to 16
- batch_rows: int32 [2, 512], P(None, 'rows'), may hold values from 0 to 127
- weights: float32 [196608, 768], P(('rows', 'labels')), may hold values from -0.21875 to 0.21875
- momentum: float32 [196608, 768], P(('rows', 'labels')), may hold values from -24 to 24
Outputs:
- new_weights: float32 [196608, 768], P(('rows', 'labels'))
- new_momentum: float32 [196608, 768], P(('rows', 'labels'))
- feature_grads: float32 [2, 512, 768], P(None, 'rows')
The draws below stay inside these ranges and needn't reach their ends.
Inputs may be any that keep to these rules, and one draw needn't show every extreme that they name: `pool_labels`: slots of a list at or past its count are padding and are ignored; a label may appear twice in a list. `batch_rows`: an entry names one of the 128 examples stored with the index of rows that owns that batch row.
All inputs are finite; a program needn't handle non-finite values.
Results may differ from the reference program's by a relative error of at most 0.00045.
The reference program's roundings to bfloat16 on the way count: a program that leaves them out, or rounds other values in their place, can miss the bound.
Values may be sent and summed in bfloat16 or wider, within the bound.
A program may use at most 64 MiB of HBM per device.

```python
import jax
import jax.numpy as jnp
from jax import lax

D = 768
LAB_DEV = 384
P_SIZE = 16
ROW_GRP = 32
POOL_ROW = 128
B = 512
LABELS = 196608
EXAMPLES = 2048


def touch_ends(array, key, low, largest):
    index_at = [jax.random.randint(jax.random.fold_in(key, axis), (), 0, length) for axis, length in enumerate(array.shape)]
    widest = array.shape.index(max(array.shape))
    next_to = index_at[:widest] + [(index_at[widest] + 1) % array.shape[widest]] + index_at[widest + 1:]
    return array.at[tuple(index_at)].set(low).at[tuple(next_to)].set(largest)


def shard_levels(rng, shape, split, smallest, top_value):
    def one(dim, blocks):
        heights = jax.random.uniform(jax.random.fold_in(jax.random.fold_in(rng, 6), dim), (blocks,), jnp.float32, smallest / len(split), top_value / len(split))
        return jnp.repeat(jnp.exp(heights), shape[dim] // blocks).reshape((-1,) + (1,) * (len(shape) - dim - 1))

    level = one(*split[0])
    for cut in split[1:]:
        level = level * one(*cut)
    return level


def scatter_about(rng, extent, spread, most, shards=(), kind=jnp.bfloat16):
    values = spread * jax.random.normal(rng, extent, jnp.float32)
    if shards:
        values = values * shard_levels(rng, extent, shards, -0.22, 0.18)
    return jnp.clip(values, -most, most).astype(kind)


def setup_inputs(seed: int = 0) -> dict:
    key_of = jax.random.split(jax.random.key(seed), 7)
    pool_features = scatter_about(key_of[0], (EXAMPLES, D), 1.0, 6.0, ((0, 16),))
    pool_labels = touch_ends(jax.random.randint(key_of[1], (EXAMPLES, P_SIZE), 0, LABELS), jax.random.fold_in(key_of[1], 1), 0, LABELS - 1).astype(jnp.int32)
    pool_counts = touch_ends(jax.random.randint(key_of[2], (EXAMPLES,), 1, P_SIZE + 1), jax.random.fold_in(key_of[2], 1), 1, P_SIZE).astype(jnp.int32)
    batch_rows = touch_ends(jax.random.randint(key_of[3], (2, B), 0, POOL_ROW), jax.random.fold_in(key_of[3], 1), 0, POOL_ROW - 1).astype(jnp.int32)
    weights = scatter_about(key_of[4], (LABELS, D), D ** -0.5, 0.21875, ((0, 512),), jnp.float32)
    momentum = scatter_about(key_of[5], (LABELS, D), 4.0, 24.0, ((0, 512),), jnp.float32)
    return {"pool_features": pool_features, "pool_labels": pool_labels, "pool_counts": pool_counts, "batch_rows": batch_rows, "weights": weights, "momentum": momentum}


learn_rate = 0.001
decay_rate = 0.9


def batch_step(features, label_ids, counts, weights, momentum):
    blocks = weights.reshape(-1, LAB_DEV, D)
    moments = momentum.reshape(-1, LAB_DEV, D)
    in_list = jnp.arange(label_ids.shape[1], dtype=jnp.int32)[None, :] < counts[:, None]

    def block_step(summed, pieces):
        weight_block, moment_block, block_index = pieces
        low_weights = weight_block.astype(jnp.bfloat16)
        logits = lax.dot_general(features, low_weights, (((1,), (1,)), ((), ())), preferred_element_type=jnp.float32)
        labels = block_index * LAB_DEV + jnp.arange(LAB_DEV, dtype=jnp.int32)
        matched = (label_ids[:, :, None] == labels[None, None, :]) & in_list[:, :, None]
        targets = jnp.any(matched, axis=1).astype(jnp.float32)
        errors = (jax.nn.sigmoid(logits) - targets).astype(jnp.bfloat16)
        grads = lax.dot_general(errors, features, (((0,), (0,)), ((), ())), preferred_element_type=jnp.float32)
        summed = summed + jnp.dot(errors, low_weights, preferred_element_type=jnp.float32)
        moment_block = decay_rate * moment_block + grads
        weight_block = weight_block - learn_rate * moment_block
        return summed, (weight_block, moment_block)

    start = jnp.zeros((features.shape[0], D), jnp.float32)
    indices = jnp.arange(blocks.shape[0], dtype=jnp.int32)
    summed, (blocks, moments) = lax.scan(block_step, start, (blocks, moments, indices))
    return summed, blocks.reshape(-1, D), moments.reshape(-1, D)


def reference(pool_features, pool_labels, pool_counts, batch_rows, weights, momentum):
    owners = (jnp.arange(B, dtype=jnp.int32) // ROW_GRP) * POOL_ROW
    results = []
    for batch in range(2):
        chosen = owners + batch_rows[batch]
        summed, weights, momentum = batch_step(pool_features[chosen], pool_labels[chosen], pool_counts[chosen], weights, momentum)
        results.append(summed)
    return weights, momentum, jnp.stack(results)
```

```python
import jax
import jax.numpy as jnp
from jax import lax
from jax.experimental import pallas as pl
from jax.experimental.pallas import tpu as pltpu
from jax.sharding import PartitionSpec as P

learn_rate = 0.001
decay_rate = 0.9
MESH = pl.DeviceIdType.MESH
F32, BF16 = jnp.float32, jnp.bfloat16

NX, NY, WIDTH, TAIL, LAB, GRP = 4, 4, 768, 128, 384, 32
FULL = WIDTH + TAIL
COUNT_LANE = 48


def one_hot(cond):
    return jnp.where(cond, 1.0, 0.0).astype(BF16)


def iota(shape, dim):
    return lax.broadcasted_iota(jnp.int32, shape, dim)


def dot(a, b, dims):
    return lax.dot_general(a, b, (dims, ((), ())), preferred_element_type=F32)


def kernel(
    pool, labels, counts, batch_rows, w_in, m_in,
    w_out, m_out, fg_out,
    feats, w, m, low, logits, errs, grads, own_part, other_part, core_in, chip_sum,
    plane_in, quarter, line_in, line_sum, far_in, result,
    x_send, x_recv, edge_send, edge_recv, core_send, core_recv, part_send, part_recv,
    plane_send, plane_recv, line_send, line_recv, far_send, far_recv, all_send, all_recv, local,
):
    rows_at, labels_at = lax.axis_index("rows"), lax.axis_index("labels")
    zh, x, c = rows_at >> 3, (rows_at >> 1) & 3, rows_at & 1
    y, zl = labels_at >> 3, labels_at & 7
    z = zh * 8 + zl
    a, b = z >> 2, z & 3
    edge = (zl == 0) | (zl == 7)
    holder = zh == (y >> 1)
    pending = []

    def device(x=x, y=y, z=z, c=c):
        z = z & 15
        return ((z >> 3) * 8 + x * 2 + c, y * 8 + (z & 7))

    def remote(src, dst, send, recv, to):
        return pltpu.make_async_remote_copy(
            src_ref=src, dst_ref=dst, send_sem=send, recv_sem=recv,
            device_id=to, device_id_type=MESH,
        )

    def start(*args, when=None):
        def go():
            remote(*args).start()

        def done():
            remote(*args).wait_send()

        pending.append((done, when))
        if when is None:
            go()
        else:
            pl.when(when)(go)

    def arrived(dst, recv):
        remote(dst, dst, recv, recv, device(c=1 - c)).wait_recv()

    barrier = pltpu.get_barrier_semaphore()

    def greet(to):
        pl.semaphore_signal(barrier, inc=1, device_id=to, device_id_type=MESH)

    source_z = jnp.where(zl < 4, zh * 8 + 15, zh * 8 + 8)
    greet(device(z=source_z))
    greet(device(c=1 - c))
    for p in range(1, 16):
        greet(device(x=(x + (p >> 2)) & 3, y=(y + (p & 3)) & 3))
    for d in range(1, 4):
        greet(device(z=a * 4 + ((b + d) & 3)))
    for i in range(2):
        for k in range(4):
            from_y = 2 * zh + i

            @pl.when((from_y != y) | (k != b))
            def _():
                greet(device(y=from_y, z=a * 4 + k))

    @pl.when(holder)
    def _():
        for d in range(1, 4):
            greet(device(z=z + 4 * d))

    load_w = pltpu.make_async_copy(w_in, w, local.at[0])
    load_m = pltpu.make_async_copy(m_in, m, local.at[1])
    load_w.start()
    load_m.start()

    lists = labels[...]
    tail = jnp.zeros((128, TAIL), F32)
    for d in range(3):
        digit = ((lists >> (6 * d)) & 63).astype(F32).astype(BF16)
        place = one_hot(iota((16, TAIL), 0) + 16 * d == iota((16, TAIL), 1))
        tail = tail + dot(digit, place, ((1,), (0,)))
    on_diagonal = iota((128, 128), 0) == iota((128, 128), 1)
    diagonal = jnp.where(on_diagonal, counts[...].astype(F32), 0.0).astype(BF16)
    tail = tail + dot(diagonal, one_hot(iota((128, TAIL), 1) == COUNT_LANE), ((1,), (0,)))
    tail = tail.astype(BF16)
    for t in range(2):
        chosen = one_hot(iota((128, GRP), 0) == batch_rows[pl.ds(t, 1), :])
        own = feats.at[t, 0, 0, x]
        own[:, :WIDTH] = dot(chosen, pool[...], ((0,), (0,))).astype(BF16)
        own[:, WIDTH:] = dot(chosen, tail, ((0,), (0,))).astype(BF16)

    pl.semaphore_wait(
        barrier, 19 + jnp.where(holder, 16, 2) + jnp.where(edge, 4, 0)
    )

    def send_edge(t):
        for k in (3, 2, 1, 0):
            to_z = jnp.where(zl == 0, z - 1 - k, z + 1 + k)
            start(
                feats.at[t, 0, 0, x], feats.at[t, 1, 0, x],
                edge_send.at[t, k], edge_recv.at[t], device(z=to_z), when=edge,
            )

    def send_core(t, far, at):
        start(
            feats.at[t, far, 0, at], feats.at[t, far, 1, at],
            core_send.at[t, far, at], core_recv.at[t, far, at], device(c=1 - c),
        )

    def send_x(t, far):
        for d in (2, 1, 3):
            start(
                feats.at[t, far, 0, x], feats.at[t, far, 0, x],
                x_send.at[t, far, d - 1], x_recv.at[t, far, d - 1], device(x=(x + d) & 3),
            )
        send_core(t, far, x)

    def pass_on(t, far):
        for d in (1, 3, 2):
            at = (x - d) & 3
            arrived(feats.at[t, far, 0, at], x_recv.at[t, far, d - 1])
            send_core(t, far, at)

    def have_edge(t):
        arrived(feats.at[t, 1, 0, x], edge_recv.at[t])
        send_x(t, 1)

    def have_core(t, far):
        for at in range(NX):
            arrived(feats.at[t, far, 1, at], core_recv.at[t, far, at])

    base = ((rows_at * 32 + labels_at) * LAB).astype(F32)

    def block_errors(t, far):
        block = feats[t, far].reshape(8 * GRP, FULL)
        features, lists = block[:, :WIDTH], block[:, WIDTH:]
        logits[...] = dot(low[t], features, ((1,), (1,)))
        slot, lane = iota((16, TAIL), 0), iota((16, TAIL), 1)
        weight = jnp.zeros((16, TAIL), F32)
        for d in range(3):
            weight = jnp.where(lane == slot + 16 * d, float(64**d), weight)
        ids = dot(weight.astype(BF16), lists, ((1,), (1,)))
        used = dot(one_hot(lane == COUNT_LANE), lists, ((1,), (1,)))
        in_list = iota(ids.shape, 0).astype(F32) < used
        ids = jnp.where(in_list, ids - base, -1.0)

        def chunk(i, _):
            at = pl.ds(pl.multiple_of(i * 64, 64), 64)
            label = (iota((64, 8 * GRP), 0) + i * 64).astype(F32)
            hit = ids[0:1, :] == label
            for k in range(1, 16):
                hit = hit | (ids[k : k + 1, :] == label)
            targets = jnp.where(hit, 1.0, 0.0)
            errs[t, far, at, :] = (jax.nn.sigmoid(logits[at, :]) - targets).astype(BF16)
            return 0

        lax.fori_loop(0, LAB // 64, chunk, 0)
        part = dot(errs[t, far], features, ((1,), (0,)))
        if far:
            grads[...] += part
        else:
            grads[...] = part

    def update(t):
        def chunk(i, _):
            at = pl.ds(pl.multiple_of(i * 64, 64), 64)
            moment = decay_rate * m[at, :] + grads[at, :]
            weight = w[at, :] - learn_rate * moment
            m[at, :] = moment
            w[at, :] = weight
            if t == 0:
                low[1, at, :] = weight.astype(BF16)
            return 0

        lax.fori_loop(0, LAB // 64, chunk, 0)

    def products(t):
        for other in (1, 0):
            cols = pl.ds(other * 128, 128)
            both = jnp.concatenate([errs[t, 0, :, cols], errs[t, 1, :, cols]], axis=1)
            part = dot(both, low[t], ((0,), (0,))).reshape(2, NX, 2, 16, WIDTH)
            if other:
                other_part[t] = part
                start(
                    other_part.at[t], core_in.at[t],
                    part_send.at[t], part_recv.at[t], device(c=1 - c),
                )
            else:
                own_part[t] = part

    def plane_start(t):
        arrived(core_in.at[t], part_recv.at[t])

        def chunk(i, _):
            far, at = i >> 2, i & 3
            chip_sum[t, far, at] = (own_part[t, far, at] + core_in[t, far, at]).astype(BF16)
            return 0

        lax.fori_loop(0, 8, chunk, 0)
        for p in range(1, 16):
            to_x, to_y = (x + (p >> 2)) & 3, (y + (p & 3)) & 3
            start(
                chip_sum.at[t, (to_y >> 1) ^ zh, to_x, to_y & 1], plane_in.at[t, p - 1],
                plane_send.at[t, p - 1], plane_recv.at[t, p - 1], device(x=to_x, y=to_y),
            )

    def line_start(t):
        mine = (t, (y >> 1) ^ zh, x, y & 1)
        total = own_part[mine] + core_in[mine]
        for p in range(1, 16):
            arrived(plane_in.at[t, p - 1], plane_recv.at[t, p - 1])
        for p in range(1, 16):
            total = total + plane_in[t, p - 1].astype(F32)
        for k in range(4):
            quarter[t, k] = total[8 * (k >> 1) : 8 * (k >> 1) + 8, 384 * (k & 1) : 384 * (k & 1) + 384]
        for d in range(1, 4):
            to_b = (b + d) & 3
            start(
                quarter.at[t, to_b], line_in.at[t, d - 1],
                line_send.at[t, d - 1], line_recv.at[t, d - 1], device(z=a * 4 + to_b),
            )

    def far_start(t):
        total = quarter[t, b]
        for d in range(1, 4):
            arrived(line_in.at[t, d - 1], line_recv.at[t, d - 1])
            total = total + line_in[t, d - 1]
        line_sum[t] = total
        for d in (2, 1, 3):
            start(
                line_sum.at[t], far_in.at[t, d - 1], far_send.at[t, d - 1], far_recv.at[t, d - 1],
                device(z=z + 4 * d), when=(((a + d) & 3) >> 1) == (y >> 1),
            )

    def all_start(t):
        @pl.when(holder)
        def _():
            total = line_sum[t]
            for d in range(1, 4):
                arrived(far_in.at[t, d - 1], far_recv.at[t, d - 1])
                total = total + far_in[t, d - 1]
            result[t, y & 1, b] = total

        for q in range(15, 0, -1):
            start(
                result.at[t, y & 1, b], result.at[t, y & 1, b],
                all_send.at[t, q - 1], all_recv.at[t, y & 1, b],
                device(y=(y + (q >> 2)) & 3, z=a * 4 + ((b + (q & 3)) & 3)), when=holder,
            )

    def finish(t):
        for i in range(2):
            for k in range(4):
                mine = holder & (i == (y & 1)) & (k == b)

                @pl.when(jnp.logical_not(mine))
                def _():
                    arrived(result.at[t, i, k], all_recv.at[t, i, k])

        for i in range(2):
            for k in range(4):
                r, s = 16 * i + 8 * (k >> 1), 384 * (k & 1)
                fg_out[t, r : r + 8, s : s + 384] = result[t, i, k]

    send_edge(0)
    send_x(0, 0)
    send_x(1, 0)
    load_w.wait()
    load_m.wait()
    low[0] = w[...].astype(BF16)
    pass_on(0, 0)
    send_edge(1)
    have_edge(0)
    have_core(0, 0)
    block_errors(0, 0)
    pass_on(1, 0)
    pass_on(0, 1)
    have_core(0, 1)
    block_errors(0, 1)
    update(0)
    have_edge(1)
    products(0)
    have_core(1, 0)
    block_errors(1, 0)
    pass_on(1, 1)
    plane_start(0)
    have_core(1, 1)
    block_errors(1, 1)
    products(1)
    line_start(0)
    plane_start(1)
    update(1)
    store_w = pltpu.make_async_copy(w, w_out, local.at[2])
    store_m = pltpu.make_async_copy(m, m_out, local.at[3])
    store_w.start()
    store_m.start()
    far_start(0)
    line_start(1)
    all_start(0)
    far_start(1)
    all_start(1)
    finish(0)
    finish(1)
    for done, when in pending:
        if when is None:
            done()
        else:
            pl.when(when)(done)
    store_w.wait()
    store_m.wait()


def per_device(pool_features, pool_labels, pool_counts, batch_rows, weights, momentum):
    vmem, anywhere = pl.BlockSpec(memory_space=pltpu.VMEM), pl.BlockSpec(memory_space=pl.ANY)
    dma = pltpu.SemaphoreType.DMA
    part = (2, 2, NX, 2, 16, WIDTH)
    return pl.pallas_call(
        kernel,
        out_shape=(
            jax.ShapeDtypeStruct(weights.shape, F32),
            jax.ShapeDtypeStruct(momentum.shape, F32),
            jax.ShapeDtypeStruct((2, GRP, WIDTH), F32),
        ),
        in_specs=[vmem, vmem, vmem, vmem, anywhere, anywhere],
        out_specs=(anywhere, anywhere, vmem),
        scratch_shapes=[
            pltpu.VMEM((2, 2, 2, NX, GRP, FULL), BF16),
            pltpu.VMEM((LAB, WIDTH), F32),
            pltpu.VMEM((LAB, WIDTH), F32),
            pltpu.VMEM((2, LAB, WIDTH), BF16),
            pltpu.VMEM((LAB, 8 * GRP), F32),
            pltpu.VMEM((2, 2, LAB, 8 * GRP), BF16),
            pltpu.VMEM((LAB, WIDTH), F32),
            pltpu.VMEM(part, F32),
            pltpu.VMEM(part, F32),
            pltpu.VMEM(part, F32),
            pltpu.VMEM(part, BF16),
            pltpu.VMEM((2, 15, 16, WIDTH), BF16),
            pltpu.VMEM((2, 4, 8, 384), F32),
            pltpu.VMEM((2, 3, 8, 384), F32),
            pltpu.VMEM((2, 8, 384), F32),
            pltpu.VMEM((2, 3, 8, 384), F32),
            pltpu.VMEM((2, 2, 4, 8, 384), F32),
            dma((2, 2, 3)), dma((2, 2, 3)),
            dma((2, 4)), dma((2,)),
            dma((2, 2, NX)), dma((2, 2, NX)),
            dma((2,)), dma((2,)),
            dma((2, 15)), dma((2, 15)),
            dma((2, 3)), dma((2, 3)),
            dma((2, 3)), dma((2, 3)),
            dma((2, 15)), dma((2, 2, 4)),
            dma((4,)),
        ],
        compiler_params=pltpu.CompilerParams(
            collective_id=0, has_side_effects=True, vmem_limit_bytes=48 << 20
        ),
    )(pool_features, pool_labels, pool_counts.reshape(1, -1), batch_rows, weights, momentum)


def solution(mesh):
    in_specs = (
        P("rows", None),
        P("rows", None),
        P("rows"),
        P(None, "rows"),
        P(("rows", "labels"), None),
        P(("rows", "labels"), None),
    )
    out_specs = (P(("rows", "labels"), None), P(("rows", "labels"), None), P(None, "rows", None))
    return jax.shard_map(
        per_device, mesh=mesh, in_specs=in_specs, out_specs=out_specs, check_vma=False
    )
```

```python
import jax
import jax.numpy as jnp
from jax import lax
from jax.experimental import pallas as pl
from jax.experimental.pallas import tpu as pltpu
from jax.sharding import PartitionSpec as P

learn_rate = 0.001
decay_rate = 0.9
MESH = pl.DeviceIdType.MESH
F32, BF16 = jnp.float32, jnp.bfloat16

NX, NY, WIDTH, TAIL, LAB, GRP = 4, 4, 768, 128, 384, 32
FULL = WIDTH + TAIL
COUNT_LANE = 48


def one_hot(cond):
    return jnp.where(cond, 1.0, 0.0).astype(BF16)


def iota(shape, dim):
    return lax.broadcasted_iota(jnp.int32, shape, dim)


def dot(a, b, dims):
    return lax.dot_general(a, b, (dims, ((), ())), preferred_element_type=F32)


def kernel(
    pool_in, labels_in, counts_in, rows_in, w_in, m_in,
    w, m, fg_out,
    pool, labels, counts, batch_rows, feats, low, logits, errs, grads, own_part, other_part, core_in, chip_sum,
    plane_in, quarter, line_in, line_sum, far_in, result,
    x_send, x_recv, edge_send, edge_recv, pair_send, pair_recv, core_send, core_recv, part_send, part_recv,
    plane_send, plane_recv, line_send, line_recv, far_send, far_recv, all_send, all_recv, local,
):
    rows_at, labels_at = lax.axis_index("rows"), lax.axis_index("labels")
    zh, x, c = rows_at >> 3, (rows_at >> 1) & 3, rows_at & 1
    y, zl = labels_at >> 3, labels_at & 7
    z = zh * 8 + zl
    a, b = z >> 2, z & 3
    edge = (zl == 0) | (zl == 7)
    holder = zh == (y >> 1)
    half = y & 1
    piece = b ^ (a & 2)
    pending = []

    def far_z(d):
        to = (a + d) & 3
        return to * 4 + (piece ^ (to & 2))

    def device(x=x, y=y, z=z, c=c):
        z = z & 15
        return ((z >> 3) * 8 + x * 2 + c, y * 8 + (z & 7))

    def remote(src, dst, send, recv, to):
        return pltpu.make_async_remote_copy(
            src_ref=src, dst_ref=dst, send_sem=send, recv_sem=recv,
            device_id=to, device_id_type=MESH,
        )

    def start(*args, when=None):
        def go():
            remote(*args).start()

        def done():
            remote(*args).wait_send()

        pending.append((done, when))
        if when is None:
            go()
        else:
            pl.when(when)(go)

    def arrived(dst, recv):
        remote(dst, dst, recv, recv, device(c=1 - c)).wait_recv()

    load_w = pltpu.make_async_copy(w_in, w, local.at[0])
    load_m = pltpu.make_async_copy(m_in, m, local.at[1])
    small = [
        pltpu.make_async_copy(src, dst, local.at[2 + i])
        for i, (src, dst) in enumerate(
            ((pool_in, pool), (labels_in, labels), (counts_in, counts), (rows_in, batch_rows))
        )
    ]
    for copy in small:
        copy.start()
    load_w.start()
    load_m.start()

    barrier = pltpu.get_barrier_semaphore()

    def greet(to):
        pl.semaphore_signal(barrier, inc=1, device_id=to, device_id_type=MESH)

    source_z = jnp.where(zl < 4, zh * 8 + 15, zh * 8 + 8)
    greet(device(z=source_z))
    greet(device(c=1 - c))
    for p in range(1, 16):
        greet(device(x=(x + (p >> 2)) & 3, y=(y + (p & 3)) & 3))
    for d in range(1, 4):
        greet(device(z=a * 4 + ((b + d) & 3)))
    for i in range(2):
        for k in range(4):
            from_y = 2 * zh + i

            @pl.when((from_y != y) | (k != b))
            def _():
                greet(device(y=from_y, z=a * 4 + k))

    @pl.when(holder)
    def _():
        for d in range(1, 4):
            greet(device(z=far_z(d)))


    for copy in small:
        copy.wait()
    lists = labels[...]
    tail = jnp.zeros((128, TAIL), F32)
    for d in range(3):
        digit = ((lists >> (6 * d)) & 63).astype(F32).astype(BF16)
        place = one_hot(iota((16, TAIL), 0) + 16 * d == iota((16, TAIL), 1))
        tail = tail + dot(digit, place, ((0,), (0,)))
    on_diagonal = iota((128, 128), 0) == iota((128, 128), 1)
    diagonal = jnp.where(on_diagonal, counts[...].astype(F32), 0.0).astype(BF16)
    tail = tail + dot(diagonal, one_hot(iota((128, TAIL), 1) == COUNT_LANE), ((1,), (0,)))
    tail = tail.astype(BF16)
    for t in range(2):
        chosen = one_hot(iota((128, GRP), 0) == batch_rows[pl.ds(t, 1), :])
        own = feats.at[t, 0, 0, x]
        features = dot(chosen, pool[...], ((0,), (0,))).astype(BF16)
        own[:, :, :WIDTH] = features.reshape(2, 16, WIDTH)
        own[:, :, WIDTH:] = dot(chosen, tail, ((0,), (0,))).astype(BF16).reshape(2, 16, TAIL)

    pl.semaphore_wait(
        barrier, 19 + jnp.where(holder, 16, 2) + jnp.where(edge, 4, 0)
    )

    def send_edge(t):
        for k in (3, 2, 1, 0):
            to_z = jnp.where(zl == 0, z - 1 - k, z + 1 + k)
            start(
                feats.at[t, 0, 0, x, half], feats.at[t, 1, 0, x, half],
                edge_send.at[t, k], edge_recv.at[t], device(z=to_z), when=edge,
            )

    def send_core(*at):
        start(
            feats.at[at[0], at[1], 0, *at[2:]], feats.at[at[0], at[1], 1, *at[2:]],
            core_send.at[*at, *[0] * (4 - len(at))], core_recv.at[*at, *[0] * (4 - len(at))],
            device(c=1 - c),
        )

    def send_x(t):
        for d in (2, 1, 3):
            start(
                feats.at[t, 0, 0, x], feats.at[t, 0, 0, x],
                x_send.at[t, d - 1], x_recv.at[t, d - 1], device(x=(x + d) & 3),
            )
        send_core(t, 0, x)

    def pass_near(t):
        for d in (1, 3, 2):
            at = (x - d) & 3
            arrived(feats.at[t, 0, 0, at], x_recv.at[t, d - 1])
            send_core(t, 0, at)

    def have_edge(t):
        arrived(feats.at[t, 1, 0, x, half], edge_recv.at[t])
        for q in (5, 4, 3, 7, 2, 6, 1):
            start(
                feats.at[t, 1, 0, x, half], feats.at[t, 1, 0, x, half],
                pair_send.at[t, q - 1], pair_recv.at[t, q - 1],
                device(x=(x + (q >> 1)) & 3, y=y ^ (q & 1)),
            )
        send_core(t, 1, x, half)

    def pass_far(t):
        for q in (1, 2, 6, 3, 7, 4, 5):
            at = (x - (q >> 1)) & 3, half ^ (q & 1)
            arrived(feats.at[t, 1, 0, *at], pair_recv.at[t, q - 1])
            send_core(t, 1, *at)

    def have_core(t, far):
        for at in range(NX):
            if far:
                for i in range(2):
                    arrived(feats.at[t, 1, 1, at, i], core_recv.at[t, 1, at, i])
            else:
                arrived(feats.at[t, 0, 1, at], core_recv.at[t, 0, at, 0])

    base = ((rows_at * 32 + labels_at) * LAB).astype(F32)

    def block_errors(t, far):
        block = feats[t, far].reshape(8 * GRP, FULL)
        features, lists = block[:, :WIDTH], block[:, WIDTH:]
        logits[...] = dot(low[t], features, ((1,), (1,)))
        slot, lane = iota((16, TAIL), 0), iota((16, TAIL), 1)
        weight = jnp.zeros((16, TAIL), F32)
        for d in range(3):
            weight = jnp.where(lane == slot + 16 * d, float(64**d), weight)
        ids = dot(weight.astype(BF16), lists, ((1,), (1,)))
        used = dot(one_hot(lane == COUNT_LANE), lists, ((1,), (1,)))
        in_list = iota(ids.shape, 0).astype(F32) < used
        ids = jnp.where(in_list, ids - base, -1.0)

        def chunk(i, _):
            at = pl.ds(pl.multiple_of(i * 64, 64), 64)
            label = (iota((64, 8 * GRP), 0) + i * 64).astype(F32)
            hit = ids[0:1, :] == label
            for k in range(1, 16):
                hit = hit | (ids[k : k + 1, :] == label)
            targets = jnp.where(hit, 1.0, 0.0)
            errs[t, far, at, :] = (jax.nn.sigmoid(logits[at, :]) - targets).astype(BF16)
            return 0

        lax.fori_loop(0, LAB // 64, chunk, 0)
        part = dot(errs[t, far], features, ((1,), (0,)))
        if far:
            grads[...] += part
        else:
            grads[...] = part

    def update(t):
        def chunk(i, _):
            at = pl.ds(pl.multiple_of(i * 64, 64), 64)
            moment = decay_rate * m[at, :] + grads[at, :]
            weight = w[at, :] - learn_rate * moment
            m[at, :] = moment
            w[at, :] = weight
            if t == 0:
                low[1, at, :] = weight.astype(BF16)
            return 0

        lax.fori_loop(0, LAB // 64, chunk, 0)

    def products(t):
        for other in (1, 0):
            cols = pl.ds(other * 128, 128)
            both = jnp.concatenate([errs[t, 0, :, cols], errs[t, 1, :, cols]], axis=1)
            part = dot(both, low[t], ((0,), (0,))).reshape(2, NX, 2, 16, WIDTH)
            if other:
                for at in range(NX):
                    other_part[t, at] = part[:, at]
                for d in (2, 1, 3, 0):
                    at = (x + d) & 3
                    start(
                        other_part.at[t, at], core_in.at[t, at],
                        part_send.at[t, at], part_recv.at[t, at], device(c=1 - c),
                    )
            else:
                for at in range(NX):
                    own_part[t, at] = part[:, at]

    def plane_start(t):
        for dx in (2, 1, 3, 0):
            to_x = (x + dx) & 3
            arrived(core_in.at[t, to_x], part_recv.at[t, to_x])
            chip_sum[t, to_x] = (own_part[t, to_x] + core_in[t, to_x]).astype(BF16)
            for dy in (2, 1, 3, 0):
                p, to_y = 4 * dx + dy, (y + dy) & 3
                if p:
                    start(
                        chip_sum.at[t, to_x, (to_y >> 1) ^ zh, to_y & 1], plane_in.at[t, p - 1],
                        plane_send.at[t, p - 1], plane_recv.at[t, p - 1], device(x=to_x, y=to_y),
                    )

    def line_start(t):
        mine = (t, x, (y >> 1) ^ zh, half)
        total = own_part[mine] + core_in[mine]
        for p in range(1, 16):
            arrived(plane_in.at[t, p - 1], plane_recv.at[t, p - 1])
        for p in range(1, 16):
            total = total + plane_in[t, p - 1].astype(F32)
        for k in range(4):
            quarter[t, k] = total[8 * (k >> 1) : 8 * (k >> 1) + 8, 384 * (k & 1) : 384 * (k & 1) + 384]
        for d in (2, 1, 3):
            to_b = (b + d) & 3
            start(
                quarter.at[t, to_b ^ (a & 2)], line_in.at[t, d - 1],
                line_send.at[t, d - 1], line_recv.at[t, d - 1], device(z=a * 4 + to_b),
            )

    def far_start(t):
        total = quarter[t, piece]
        for d in range(1, 4):
            arrived(line_in.at[t, d - 1], line_recv.at[t, d - 1])
            total = total + line_in[t, d - 1]
        line_sum[t] = total
        for d in (2, 1, 3):
            start(
                line_sum.at[t], far_in.at[t, d - 1], far_send.at[t, d - 1], far_recv.at[t, d - 1],
                device(z=far_z(d)), when=(((a + d) & 3) >> 1) == (y >> 1),
            )

    def all_start(t):
        @pl.when(holder)
        def _():
            total = line_sum[t]
            for d in range(1, 4):
                arrived(far_in.at[t, d - 1], far_recv.at[t, d - 1])
                total = total + far_in[t, d - 1]
            result[t, half, piece] = total

        for q in range(15, 0, -1):
            start(
                result.at[t, half, piece], result.at[t, half, piece],
                all_send.at[t, q - 1], all_recv.at[t, half, piece],
                device(y=(y + (q >> 2)) & 3, z=a * 4 + ((b + (q & 3)) & 3)), when=holder,
            )

    def finish(t):
        for i in range(2):
            for k in range(4):
                mine = holder & (i == half) & (k == piece)

                @pl.when(jnp.logical_not(mine))
                def _():
                    arrived(result.at[t, i, k], all_recv.at[t, i, k])

        for i in range(2):
            for k in range(4):
                r, s = 16 * i + 8 * (k >> 1), 384 * (k & 1)
                fg_out[t, r : r + 8, s : s + 384] = result[t, i, k]

    send_edge(0)
    send_x(0)
    send_edge(1)
    send_x(1)
    load_w.wait()
    load_m.wait()
    low[0] = w[...].astype(BF16)
    pass_near(0)
    have_edge(0)
    have_core(0, 0)
    block_errors(0, 0)
    pass_near(1)
    pass_far(0)
    have_core(0, 1)
    block_errors(0, 1)
    update(0)
    have_edge(1)
    products(0)
    have_core(1, 0)
    block_errors(1, 0)
    pass_far(1)
    plane_start(0)
    have_core(1, 1)
    block_errors(1, 1)
    products(1)
    plane_start(1)
    line_start(0)
    update(1)
    far_start(0)
    line_start(1)
    all_start(0)
    far_start(1)
    all_start(1)
    finish(0)
    finish(1)
    for done, when in pending:
        if when is None:
            done()
        else:
            pl.when(when)(done)


def store(w, m, fg, w_out, m_out, fg_out, sems):
    copies = [pltpu.make_async_copy(fg, fg_out, sems.at[0])]
    for src, dst in ((w, w_out), (m, m_out)):
        for i in range(4):
            at = pl.ds(i * (LAB // 4), LAB // 4)
            copies.append(pltpu.make_async_copy(src.at[at], dst.at[at], sems.at[len(copies)]))
    for copy in copies:
        copy.start()
    for copy in copies:
        copy.wait()


def per_device(pool_features, pool_labels, pool_counts, batch_rows, weights, momentum):
    vmem, hbm = pl.BlockSpec(memory_space=pltpu.VMEM), pl.BlockSpec(memory_space=pltpu.HBM)
    dma = pltpu.SemaphoreType.DMA
    part = (2, NX, 2, 2, 16, WIDTH)
    shapes = (
        jax.ShapeDtypeStruct(weights.shape, F32),
        jax.ShapeDtypeStruct(momentum.shape, F32),
        jax.ShapeDtypeStruct((2, GRP, WIDTH), F32),
    )
    results = pl.pallas_call(
        kernel,
        out_shape=tuple(pltpu.VMEM(s.shape, s.dtype) for s in shapes),
        in_specs=[hbm] * 6,
        out_specs=(vmem, vmem, vmem),
        scratch_shapes=[
            pltpu.VMEM((128, WIDTH), BF16),
            pltpu.VMEM((16, 128), jnp.int32),
            pltpu.VMEM((1, 128), jnp.int32),
            pltpu.VMEM((2, GRP), jnp.int32),
            pltpu.VMEM((2, 2, 2, NX, 2, 16, FULL), BF16),
            pltpu.VMEM((2, LAB, WIDTH), BF16),
            pltpu.VMEM((LAB, 8 * GRP), F32),
            pltpu.VMEM((2, 2, LAB, 8 * GRP), BF16),
            pltpu.VMEM((LAB, WIDTH), F32),
            pltpu.VMEM(part, F32),
            pltpu.VMEM(part, F32),
            pltpu.VMEM(part, F32),
            pltpu.VMEM(part, BF16),
            pltpu.VMEM((2, 15, 16, WIDTH), BF16),
            pltpu.VMEM((2, 4, 8, 384), F32),
            pltpu.VMEM((2, 3, 8, 384), F32),
            pltpu.VMEM((2, 8, 384), F32),
            pltpu.VMEM((2, 3, 8, 384), F32),
            pltpu.VMEM((2, 2, 4, 8, 384), F32),
            dma((2, 3)), dma((2, 3)),
            dma((2, 4)), dma((2,)),
            dma((2, 7)), dma((2, 7)),
            dma((2, 2, NX, 2)), dma((2, 2, NX, 2)),
            dma((2, NX)), dma((2, NX)),
            dma((2, 15)), dma((2, 15)),
            dma((2, 3)), dma((2, 3)),
            dma((2, 3)), dma((2, 3)),
            dma((2, 15)), dma((2, 2, 4)),
            dma((6,)),
        ],
        compiler_params=pltpu.CompilerParams(
            collective_id=0, has_side_effects=True, vmem_limit_bytes=48 << 20
        ),
    )(
        *(
            pltpu.with_memory_space_constraint(array, pltpu.HBM)
            for array in (
                pool_features, pool_labels.T, pool_counts.reshape(1, -1), batch_rows,
                weights, momentum,
            )
        )
    )
    return pl.pallas_call(
        store,
        out_shape=shapes,
        in_specs=[vmem] * 3,
        out_specs=(hbm,) * 3,
        scratch_shapes=[dma((9,))],
    )(*(pltpu.with_memory_space_constraint(array, pltpu.VMEM) for array in results))


def solution(mesh):
    in_specs = (
        P("rows", None),
        P("rows", None),
        P("rows"),
        P(None, "rows"),
        P(("rows", "labels"), None),
        P(("rows", "labels"), None),
    )
    out_specs = (P(("rows", "labels"), None), P(("rows", "labels"), None), P(None, "rows", None))
    return jax.shard_map(
        per_device, mesh=mesh, in_specs=in_specs, out_specs=out_specs, check_vma=False
    )
```

```python
import jax
import jax.numpy as jnp
from jax import lax
from jax.experimental import pallas as pl
from jax.experimental.pallas import tpu as pltpu
from jax.sharding import PartitionSpec as P

learn_rate = 0.001
decay_rate = 0.9
MESH = pl.DeviceIdType.MESH
F32, BF16 = jnp.float32, jnp.bfloat16

NX, NY, WIDTH, TAIL, LAB, GRP = 4, 4, 768, 128, 384, 32
FULL = WIDTH + TAIL
COUNT_LANE = 48


def one_hot(cond):
    return jnp.where(cond, 1.0, 0.0).astype(BF16)


def iota(shape, dim):
    return lax.broadcasted_iota(jnp.int32, shape, dim)


def dot(a, b, dims):
    return lax.dot_general(a, b, (dims, ((), ())), preferred_element_type=F32)


def kernel(
    pool_in, labels_in, counts_in, rows_in, w_in, m_in,
    w, m, fg_out,
    pool, labels, counts, batch_rows, feats0, feats1, low, logits, errs, grads, own_part, other_part, core_in, chip_sum,
    plane_in, quarter, line_in, line_sum, far_in, result,
    x_send, x_recv, edge_send, edge_recv, pair_send, pair_recv, core_send, core_recv, part_send, part_recv,
    plane_send, plane_recv, line_send, line_recv, far_send, far_recv, all_send, all_recv, local,
):
    rows_at, labels_at = lax.axis_index("rows"), lax.axis_index("labels")
    zh, x, c = rows_at >> 3, (rows_at >> 1) & 3, rows_at & 1
    y, zl = labels_at >> 3, labels_at & 7
    z = zh * 8 + zl
    a, b = z >> 2, z & 3
    edge = (zl == 0) | (zl == 7)
    holder = zh == (y & 1)
    half, part = y & 1, y >> 1
    piece = b ^ (a & 2)
    pending = []
    feats = (feats0, feats1)

    def far_z(d):
        to = (a + d) & 3
        return to * 4 + (piece ^ (to & 2))

    def device(x=x, y=y, z=z, c=c):
        z = z & 15
        return ((z >> 3) * 8 + x * 2 + c, y * 8 + (z & 7))

    def remote(src, dst, send, recv, to):
        return pltpu.make_async_remote_copy(
            src_ref=src, dst_ref=dst, send_sem=send, recv_sem=recv,
            device_id=to, device_id_type=MESH,
        )

    def start(*args, when=None):
        def go():
            remote(*args).start()

        def done():
            remote(*args).wait_send()

        pending.append((done, when))
        if when is None:
            go()
        else:
            pl.when(when)(go)

    def arrived(dst, recv):
        remote(dst, dst, recv, recv, device(c=1 - c)).wait_recv()

    load_w = pltpu.make_async_copy(w_in, w, local.at[0])
    load_m = pltpu.make_async_copy(m_in, m, local.at[1])
    small = [
        pltpu.make_async_copy(src, dst, local.at[2 + i])
        for i, (src, dst) in enumerate(
            ((pool_in, pool), (labels_in, labels), (counts_in, counts), (rows_in, batch_rows))
        )
    ]
    for copy in small:
        copy.start()
    load_w.start()
    load_m.start()

    barrier = pltpu.get_barrier_semaphore()

    def greet(to):
        pl.semaphore_signal(barrier, inc=1, device_id=to, device_id_type=MESH)

    @pl.when(holder)
    def _():
        for d in (2, 1, 3):
            greet(device(z=far_z(d)))

    for k in range(4):
        for i in range(2):
            from_y = zh + 2 * i

            @pl.when((from_y != y) | (k != b))
            def _():
                greet(device(y=from_y, z=a * 4 + k))

    for dx in (2, 1, 3, 0):
        for dy in (2, 1, 3, 0):
            if dx or dy:
                greet(device(x=(x + dx) & 3, y=(y + dy) & 3))
    source_z = jnp.where(zl < 4, zh * 8 + 15, zh * 8 + 8)
    greet(device(z=source_z))
    for d in range(1, 4):
        greet(device(z=a * 4 + ((b + d) & 3)))
    greet(device(c=1 - c))

    for copy in small:
        copy.wait()
    lists = labels[...]
    tail = jnp.zeros((128, TAIL), F32)
    for d in range(3):
        digit = ((lists >> (6 * d)) & 63).astype(F32).astype(BF16)
        lane = iota((16, TAIL), 1) & 63
        place = one_hot(iota((16, TAIL), 0) + 16 * d == lane)
        tail = tail + dot(digit, place, ((0,), (0,)))
    on_diagonal = iota((128, 128), 0) == iota((128, 128), 1)
    diagonal = jnp.where(on_diagonal, counts[...].astype(F32), 0.0).astype(BF16)
    at_count = one_hot((iota((128, TAIL), 1) & 63) == COUNT_LANE)
    tail = (tail + dot(diagonal, at_count, ((1,), (0,)))).astype(BF16)
    chosen = [
        one_hot(iota((128, GRP), 0) == batch_rows[pl.ds(t, 1), :]) for t in range(2)
    ]
    for t in range(2):
        features = dot(chosen[t], pool[...], ((0,), (0,))).astype(BF16)
        feats[t][0, 0, x, :, :, :WIDTH] = features.reshape(2, 16, WIDTH)
    lists = [dot(chosen[t], tail, ((0,), (0,))) for t in range(2)]
    lists = jnp.where(iota((GRP, TAIL), 1) < 64, lists[0], lists[1]).astype(BF16)
    feats0[0, 0, x, :, :, WIDTH:] = lists.reshape(2, 16, TAIL)

    pl.semaphore_wait(
        barrier, 19 + jnp.where(holder, 16, 2) + jnp.where(edge, 4, 0)
    )

    def send_edge(t):
        for k in (3, 2, 1, 0):
            to_z = jnp.where(zl == 0, z - 1 - k, z + 1 + k)
            start(
                feats[t].at[0, 0, x, half], feats[t].at[1, 0, x, half],
                edge_send.at[t, k], edge_recv.at[t], device(z=to_z), when=edge,
            )

    def send_core(*at):
        start(
            feats[at[0]].at[at[1], 0, *at[2:]], feats[at[0]].at[at[1], 1, *at[2:]],
            core_send.at[*at, *[0] * (4 - len(at))], core_recv.at[*at, *[0] * (4 - len(at))],
            device(c=1 - c),
        )

    def send_x(t):
        for d in (2, 1, 3):
            start(
                feats[t].at[0, 0, x], feats[t].at[0, 0, x],
                x_send.at[t, d - 1], x_recv.at[t, d - 1], device(x=(x + d) & 3),
            )
        send_core(t, 0, x)

    def pass_near(t):
        for d in (1, 3, 2):
            at = (x - d) & 3
            arrived(feats[t].at[0, 0, at], x_recv.at[t, d - 1])
            send_core(t, 0, at)

    def have_edge(t):
        arrived(feats[t].at[1, 0, x, half], edge_recv.at[t])
        for q in (5, 4, 3, 7, 2, 6, 1):
            start(
                feats[t].at[1, 0, x, half], feats[t].at[1, 0, x, half],
                pair_send.at[t, q - 1], pair_recv.at[t, q - 1],
                device(x=(x + (q >> 1)) & 3, y=y ^ (q & 1)),
            )
        send_core(t, 1, x, half)

    def pass_far(t):
        for q in (1, 2, 6, 3, 7, 4, 5):
            at = (x - (q >> 1)) & 3, half ^ (q & 1)
            arrived(feats[t].at[1, 0, *at], pair_recv.at[t, q - 1])
            send_core(t, 1, *at)

    def have_core(t, far):
        for at in range(NX):
            if far:
                for i in range(2):
                    arrived(feats[t].at[1, 1, at, i], core_recv.at[t, 1, at, i])
            else:
                arrived(feats[t].at[0, 1, at], core_recv.at[t, 0, at, 0])

    base = ((rows_at * 32 + labels_at) * LAB).astype(F32)

    def block_errors(t, far):
        features = feats[t][far, :, :, :, :, :WIDTH].reshape(8 * GRP, WIDTH)
        lists = feats0[far, :, :, :, :, WIDTH:].reshape(8 * GRP, TAIL)
        logits[...] = dot(low[t], features, ((1,), (1,)))
        slot, lane = iota((16, TAIL), 0), iota((16, TAIL), 1) - 64 * t
        weight = jnp.zeros((16, TAIL), F32)
        for d in range(3):
            weight = jnp.where(lane == slot + 16 * d, float(64**d), weight)
        ids = dot(weight.astype(BF16), lists, ((1,), (1,)))
        used = dot(one_hot(lane == COUNT_LANE), lists, ((1,), (1,)))
        in_list = iota(ids.shape, 0).astype(F32) < used
        ids = jnp.where(in_list, ids - base, -1.0)

        def chunk(i, _):
            at = pl.ds(pl.multiple_of(i * 64, 64), 64)
            label = (iota((64, 8 * GRP), 0) + i * 64).astype(F32)
            hit = ids[0:1, :] == label
            for k in range(1, 16):
                hit = hit | (ids[k : k + 1, :] == label)
            targets = jnp.where(hit, 1.0, 0.0)
            errs[t, far, at, :] = (jax.nn.sigmoid(logits[at, :]) - targets).astype(BF16)
            return 0

        lax.fori_loop(0, LAB // 64, chunk, 0)
        part = dot(errs[t, far], features, ((1,), (0,)))
        if far:
            grads[...] += part
        else:
            grads[...] = part

    def update(t):
        def chunk(i, _):
            at = pl.ds(pl.multiple_of(i * 64, 64), 64)
            moment = decay_rate * m[at, :] + grads[at, :]
            weight = w[at, :] - learn_rate * moment
            m[at, :] = moment
            w[at, :] = weight
            if t == 0:
                low[1, at, :] = weight.astype(BF16)
            return 0

        lax.fori_loop(0, LAB // 64, chunk, 0)

    def products(t, far):
        for other in (1, 0):
            cols = pl.ds(other * 128, 128)
            product = dot(errs[t, far, :, cols], low[t], ((0,), (0,)))
            product = product.reshape(NX, 2, 16, WIDTH)
            if other:
                other_part[t, far] = product
                for d in (2, 1, 3, 0):
                    at = t, far, (x + d) & 3
                    start(
                        other_part.at[*at], core_in.at[*at],
                        part_send.at[*at], part_recv.at[*at], device(c=1 - c),
                    )
            else:
                own_part[t, far] = product

    def plane_start(t, far):
        for dx in (2, 1, 3, 0):
            to_x = (x + dx) & 3
            at = t, far, to_x
            arrived(core_in.at[*at], part_recv.at[*at])
            chip_sum[*at] = (own_part[*at] + core_in[*at]).astype(BF16)
            for i in range(2):
                to_y = (zh ^ far) + 2 * i
                slot = 4 * dx + ((to_y - y) & 3)
                start(
                    chip_sum.at[*at, i], plane_in.at[t, slot],
                    plane_send.at[t, far, 2 * dx + i], plane_recv.at[t, slot],
                    device(x=to_x, y=to_y), when=None if dx else to_y != y,
                )

    def line_start(t):
        mine = (t, half ^ zh, x, part)
        total = own_part[mine] + core_in[mine]
        for p in range(1, 16):
            arrived(plane_in.at[t, p], plane_recv.at[t, p])
        for p in range(1, 16):
            total = total + plane_in[t, p].astype(F32)
        for k in range(4):
            r, col = 8 * (k >> 1), 384 * (k & 1)
            quarter[t, k] = total[r : r + 8, col : col + 384]
        for d in (2, 1, 3):
            to_b = (b + d) & 3
            start(
                quarter.at[t, to_b ^ (a & 2)], line_in.at[t, d - 1],
                line_send.at[t, d - 1], line_recv.at[t, d - 1], device(z=a * 4 + to_b),
            )

    def far_start(t):
        total = quarter[t, piece]
        for d in range(1, 4):
            arrived(line_in.at[t, d - 1], line_recv.at[t, d - 1])
            total = total + line_in[t, d - 1]
        line_sum[t] = total
        for d in (2, 1, 3):
            start(
                line_sum.at[t], far_in.at[t, d - 1], far_send.at[t, d - 1], far_recv.at[t, d - 1],
                device(z=far_z(d)), when=(((a + d) & 3) >> 1) == (y & 1),
            )

    def all_start(t):
        @pl.when(holder)
        def _():
            total = line_sum[t]
            for d in range(1, 4):
                arrived(far_in.at[t, d - 1], far_recv.at[t, d - 1])
                total = total + far_in[t, d - 1]
            result[t, part, piece] = total

        for q in range(15, 0, -1):
            start(
                result.at[t, part, piece], result.at[t, part, piece],
                all_send.at[t, q - 1], all_recv.at[t, part, piece],
                device(y=(y + (q >> 2)) & 3, z=a * 4 + ((b + (q & 3)) & 3)), when=holder,
            )

    def finish(t):
        for i in range(2):
            for k in range(4):
                mine = holder & (i == part) & (k == piece)

                @pl.when(jnp.logical_not(mine))
                def _():
                    arrived(result.at[t, i, k], all_recv.at[t, i, k])

                r, col = 16 * i + 8 * (k >> 1), 384 * (k & 1)
                fg_out[t, r : r + 8, col : col + 384] = result[t, i, k]

    send_edge(0)
    send_x(0)
    send_edge(1)
    send_x(1)
    load_w.wait()
    load_m.wait()
    low[0] = w[...].astype(BF16)
    pass_near(0)
    have_edge(0)
    have_core(0, 0)
    block_errors(0, 0)
    pass_near(1)
    have_edge(1)
    products(0, 0)
    plane_start(0, 0)
    pass_far(0)
    have_core(0, 1)
    block_errors(0, 1)
    update(0)
    products(0, 1)
    pass_far(1)
    have_core(1, 0)
    block_errors(1, 0)
    plane_start(0, 1)
    products(1, 0)
    have_core(1, 1)
    block_errors(1, 1)
    plane_start(1, 0)
    products(1, 1)
    plane_start(1, 1)
    update(1)
    line_start(0)
    line_start(1)
    far_start(0)
    far_start(1)
    all_start(0)
    all_start(1)
    finish(0)
    finish(1)
    for done, when in pending:
        if when is None:
            done()
        else:
            pl.when(when)(done)


def store(w, m, fg, w_out, m_out, fg_out, sems):
    copies = [pltpu.make_async_copy(fg, fg_out, sems.at[0])]
    for src, dst in ((w, w_out), (m, m_out)):
        for i in range(4):
            at = pl.ds(i * (LAB // 4), LAB // 4)
            copies.append(pltpu.make_async_copy(src.at[at], dst.at[at], sems.at[len(copies)]))
    for copy in copies:
        copy.start()
    for copy in copies:
        copy.wait()


def per_device(pool_features, pool_labels, pool_counts, batch_rows, weights, momentum):
    vmem, hbm = pl.BlockSpec(memory_space=pltpu.VMEM), pl.BlockSpec(memory_space=pltpu.HBM)
    dma = pltpu.SemaphoreType.DMA
    part = (2, 2, NX, 2, 16, WIDTH)
    shapes = (
        jax.ShapeDtypeStruct(weights.shape, F32),
        jax.ShapeDtypeStruct(momentum.shape, F32),
        jax.ShapeDtypeStruct((2, GRP, WIDTH), F32),
    )
    results = pl.pallas_call(
        kernel,
        out_shape=tuple(pltpu.VMEM(s.shape, s.dtype) for s in shapes),
        in_specs=[hbm] * 6,
        out_specs=(vmem, vmem, vmem),
        scratch_shapes=[
            pltpu.VMEM((128, WIDTH), BF16),
            pltpu.VMEM((16, 128), jnp.int32),
            pltpu.VMEM((1, 128), jnp.int32),
            pltpu.VMEM((2, GRP), jnp.int32),
            pltpu.VMEM((2, 2, NX, 2, 16, FULL), BF16),
            pltpu.VMEM((2, 2, NX, 2, 16, WIDTH), BF16),
            pltpu.VMEM((2, LAB, WIDTH), BF16),
            pltpu.VMEM((LAB, 8 * GRP), F32),
            pltpu.VMEM((2, 2, LAB, 8 * GRP), BF16),
            pltpu.VMEM((LAB, WIDTH), F32),
            pltpu.VMEM(part, F32),
            pltpu.VMEM(part, F32),
            pltpu.VMEM(part, F32),
            pltpu.VMEM(part, BF16),
            pltpu.VMEM((2, 16, 16, WIDTH), BF16),
            pltpu.VMEM((2, 4, 8, 384), F32),
            pltpu.VMEM((2, 3, 8, 384), F32),
            pltpu.VMEM((2, 8, 384), F32),
            pltpu.VMEM((2, 3, 8, 384), F32),
            pltpu.VMEM((2, 2, 4, 8, 384), F32),
            dma((2, 3)), dma((2, 3)),
            dma((2, 4)), dma((2,)),
            dma((2, 7)), dma((2, 7)),
            dma((2, 2, NX, 2)), dma((2, 2, NX, 2)),
            dma((2, 2, NX)), dma((2, 2, NX)),
            dma((2, 2, 8)), dma((2, 16)),
            dma((2, 3)), dma((2, 3)),
            dma((2, 3)), dma((2, 3)),
            dma((2, 15)), dma((2, 2, 4)),
            dma((6,)),
        ],
        compiler_params=pltpu.CompilerParams(
            collective_id=0, has_side_effects=True, vmem_limit_bytes=48 << 20
        ),
    )(
        *(
            pltpu.with_memory_space_constraint(array, pltpu.HBM)
            for array in (
                pool_features, pool_labels.T, pool_counts.reshape(1, -1), batch_rows,
                weights, momentum,
            )
        )
    )
    return pl.pallas_call(
        store,
        out_shape=shapes,
        in_specs=[vmem] * 3,
        out_specs=(hbm,) * 3,
        scratch_shapes=[dma((9,))],
    )(*(pltpu.with_memory_space_constraint(array, pltpu.VMEM) for array in results))


def solution(mesh):
    in_specs = (
        P("rows", None),
        P("rows", None),
        P("rows"),
        P(None, "rows"),
        P(("rows", "labels"), None),
        P(("rows", "labels"), None),
    )
    out_specs = (P(("rows", "labels"), None), P(("rows", "labels"), None), P(None, "rows", None))
    return jax.shard_map(
        per_device, mesh=mesh, in_specs=in_specs, out_specs=out_specs, check_vma=False
    )
```

```python
import jax
import jax.numpy as jnp
from jax import lax
from jax.experimental import pallas as pl
from jax.experimental.pallas import tpu as pltpu
from jax.sharding import PartitionSpec as P

learn_rate = 0.001
decay_rate = 0.9
MESH = pl.DeviceIdType.MESH
F32, BF16 = jnp.float32, jnp.bfloat16

NX, NY, WIDTH, TAIL, LAB, GRP = 4, 4, 768, 128, 384, 32
FULL = WIDTH + TAIL
COUNT_LANE = 48


def one_hot(cond):
    return jnp.where(cond, 1.0, 0.0).astype(BF16)


def iota(shape, dim):
    return lax.broadcasted_iota(jnp.int32, shape, dim)


def dot(a, b, dims):
    return lax.dot_general(a, b, (dims, ((), ())), preferred_element_type=F32)


def kernel(
    pool_in, labels_in, counts_in, rows_in, w_in, m_in,
    w, m, fg_out,
    pool, labels, counts, batch_rows, feats0, feats1, low, logits, errs, grads, own_part, other_part, core_in, chip_sum,
    plane_in, quarter, line_in, line_sum, far_in, result,
    x_send, x_recv, edge_send, edge_recv, pair_send, pair_recv, core_send, core_recv, part_send, part_recv,
    plane_send, plane_recv, line_send, line_recv, far_send, far_recv, all_send, all_recv, local, token,
):
    rows_at, labels_at = lax.axis_index("rows"), lax.axis_index("labels")
    zh, x, c = rows_at >> 3, (rows_at >> 1) & 3, rows_at & 1
    y, zl = labels_at >> 3, labels_at & 7
    z = zh * 8 + zl
    a, b = z >> 2, z & 3
    edge = (zl == 0) | (zl == 7)
    inner = (zl == 3) | (zl == 4)
    next_line = zh * 8 + 7 - zl
    holder = zh == (y & 1)
    half, part = y & 1, y >> 1
    piece = b ^ (a & 2)
    pending = []
    feats = (feats0, feats1)

    def far_z(d):
        to = (a + d) & 3
        return to * 4 + (piece ^ (to & 2))

    def device(x=x, y=y, z=z, c=c):
        z = z & 15
        return ((z >> 3) * 8 + x * 2 + c, y * 8 + (z & 7))

    def remote(src, dst, send, recv, to):
        return pltpu.make_async_remote_copy(
            src_ref=src, dst_ref=dst, send_sem=send, recv_sem=recv,
            device_id=to, device_id_type=MESH,
        )

    def start(*args, when=None):
        def go():
            remote(*args).start()

        def done():
            remote(*args).wait_send()

        pending.append((done, when))
        if when is None:
            go()
        else:
            pl.when(when)(go)

    def arrived(dst, recv):
        remote(dst, dst, recv, recv, device(c=1 - c)).wait_recv()

    load_w = pltpu.make_async_copy(w_in, w, local.at[0])
    load_m = pltpu.make_async_copy(m_in, m, local.at[1])
    small = [
        pltpu.make_async_copy(src, dst, local.at[2 + i])
        for i, (src, dst) in enumerate(
            ((pool_in, pool), (labels_in, labels), (counts_in, counts), (rows_in, batch_rows))
        )
    ]
    for copy in small:
        copy.start()
    load_w.start()
    load_m.start()

    barrier = pltpu.get_barrier_semaphore()

    def greet(to):
        pl.semaphore_signal(barrier, inc=1, device_id=to, device_id_type=MESH)

    for d in (2, 1, 3):
        greet(device(z=a * 4 + ((b + d) & 3)))
    for d in (2, 1, 3):
        greet(device(x=(x + d) & 3))
        greet(device(y=(y + d) & 3))
    source_z = jnp.where(zl < 4, zh * 8 + 15, zh * 8 + 8)
    greet(device(z=source_z))
    greet(device(c=1 - c))

    @pl.when(inner)
    def _():
        greet(device(z=next_line))

    for copy in small:
        copy.wait()
    lists = labels[...]
    tail = jnp.zeros((128, TAIL), F32)
    for d in range(3):
        digit = ((lists >> (6 * d)) & 63).astype(F32).astype(BF16)
        lane = iota((16, TAIL), 1) & 63
        place = one_hot(iota((16, TAIL), 0) + 16 * d == lane)
        tail = tail + dot(digit, place, ((0,), (0,)))
    on_diagonal = iota((128, 128), 0) == iota((128, 128), 1)
    diagonal = jnp.where(on_diagonal, counts[...].astype(F32), 0.0).astype(BF16)
    at_count = one_hot((iota((128, TAIL), 1) & 63) == COUNT_LANE)
    tail = (tail + dot(diagonal, at_count, ((1,), (0,)))).astype(BF16)
    chosen = [
        one_hot(iota((128, GRP), 0) == batch_rows[pl.ds(t, 1), :]) for t in range(2)
    ]
    for t in range(2):
        features = dot(chosen[t], pool[...], ((0,), (0,))).astype(BF16)
        feats[t][0, 0, x, :, :, :WIDTH] = features.reshape(2, 16, WIDTH)
    lists = [dot(chosen[t], tail, ((0,), (0,))) for t in range(2)]
    lists = jnp.where(iota((GRP, TAIL), 1) < 64, lists[0], lists[1]).astype(BF16)
    feats0[0, 0, x, :, :, WIDTH:] = lists.reshape(2, 16, TAIL)

    pl.semaphore_wait(
        barrier, 10 + jnp.where(edge, 4, 0) + jnp.where(inner, 1, 0)
    )

    def send_edge(t):
        for k in (3, 2, 1, 0):
            to_z = jnp.where(zl == 0, z - 1 - k, z + 1 + k)
            start(
                feats[t].at[0, 0, x, half], feats[t].at[1, 0, x, half],
                edge_send.at[t, k], edge_recv.at[t], device(z=to_z), when=edge,
            )

    def send_core(*at):
        start(
            feats[at[0]].at[at[1], 0, *at[2:]], feats[at[0]].at[at[1], 1, *at[2:]],
            core_send.at[*at, *[0] * (4 - len(at))], core_recv.at[*at, *[0] * (4 - len(at))],
            device(c=1 - c),
        )

    def send_x(t):
        for d in (2, 1, 3):
            start(
                feats[t].at[0, 0, x], feats[t].at[0, 0, x],
                x_send.at[t, d - 1], x_recv.at[t, d - 1], device(x=(x + d) & 3),
            )
        send_core(t, 0, x)

    def pass_near(t):
        for d in (1, 3, 2):
            at = (x - d) & 3
            arrived(feats[t].at[0, 0, at], x_recv.at[t, d - 1])
            send_core(t, 0, at)

    def have_edge(t):
        arrived(feats[t].at[1, 0, x, half], edge_recv.at[t])
        for q in (5, 4, 3, 7, 2, 6, 1):
            start(
                feats[t].at[1, 0, x, half], feats[t].at[1, 0, x, half],
                pair_send.at[t, q - 1], pair_recv.at[t, q - 1],
                device(x=(x + (q >> 1)) & 3, y=y ^ (q & 1)),
            )
        send_core(t, 1, x, half)

    def pass_far(t):
        for q in (1, 2, 6, 3, 7, 4, 5):
            at = (x - (q >> 1)) & 3, half ^ (q & 1)
            arrived(feats[t].at[1, 0, *at], pair_recv.at[t, q - 1])
            send_core(t, 1, *at)

    def send_token():
        @pl.when(inner)
        def _():
            pl.semaphore_signal(
                token.at[0], inc=1, device_id=device(z=next_line), device_id_type=MESH
            )

    def pass_token():
        @pl.when(inner)
        def _():
            pl.semaphore_wait(token.at[0], 1)
            for d in (2, 1, 3):
                pl.semaphore_signal(
                    token.at[1], inc=1, device_id=device(z=a * 4 + ((b + d) & 3)),
                    device_id_type=MESH,
                )

    def have_token():
        @pl.when(jnp.logical_not(inner))
        def _():
            pl.semaphore_wait(token.at[1], 1)

    def have_core(t, far):
        for at in range(NX):
            if far:
                for i in range(2):
                    arrived(feats[t].at[1, 1, at, i], core_recv.at[t, 1, at, i])
            else:
                arrived(feats[t].at[0, 1, at], core_recv.at[t, 0, at, 0])

    base = ((rows_at * 32 + labels_at) * LAB).astype(F32)

    def block_errors(t, far):
        features = feats[t][far, :, :, :, :, :WIDTH].reshape(8 * GRP, WIDTH)
        lists = feats0[far, :, :, :, :, WIDTH:].reshape(8 * GRP, TAIL)
        logits[...] = dot(low[t], features, ((1,), (1,)))
        slot, lane = iota((16, TAIL), 0), iota((16, TAIL), 1) - 64 * t
        weight = jnp.zeros((16, TAIL), F32)
        for d in range(3):
            weight = jnp.where(lane == slot + 16 * d, float(64**d), weight)
        ids = dot(weight.astype(BF16), lists, ((1,), (1,)))
        used = dot(one_hot(lane == COUNT_LANE), lists, ((1,), (1,)))
        in_list = iota(ids.shape, 0).astype(F32) < used
        ids = jnp.where(in_list, ids - base, -1.0)

        def chunk(i, _):
            at = pl.ds(pl.multiple_of(i * 64, 64), 64)
            label = (iota((64, 8 * GRP), 0) + i * 64).astype(F32)
            hit = ids[0:1, :] == label
            for k in range(1, 16):
                hit = hit | (ids[k : k + 1, :] == label)
            targets = jnp.where(hit, 1.0, 0.0)
            errs[t, far, at, :] = (jax.nn.sigmoid(logits[at, :]) - targets).astype(BF16)
            return 0

        lax.fori_loop(0, LAB // 64, chunk, 0)
        part = dot(errs[t, far], features, ((1,), (0,)))
        if far:
            grads[...] += part
        else:
            grads[...] = part

    def update(t):
        def chunk(i, _):
            at = pl.ds(pl.multiple_of(i * 64, 64), 64)
            moment = decay_rate * m[at, :] + grads[at, :]
            weight = w[at, :] - learn_rate * moment
            m[at, :] = moment
            w[at, :] = weight
            if t == 0:
                low[1, at, :] = weight.astype(BF16)
            return 0

        lax.fori_loop(0, LAB // 64, chunk, 0)

    def products(t, far):
        for other in (1, 0):
            cols = pl.ds(other * 128, 128)
            product = dot(errs[t, far, :, cols], low[t], ((0,), (0,)))
            product = product.reshape(NX, 2, 16, WIDTH)
            if other:
                other_part[t, far] = product
                for d in (2, 1, 3, 0):
                    at = t, far, (x + d) & 3
                    start(
                        other_part.at[*at], core_in.at[*at],
                        part_send.at[*at], part_recv.at[*at], device(c=1 - c),
                    )
            else:
                own_part[t, far] = product

    def plane_start(t, far):
        for dx in (2, 1, 3, 0):
            to_x = (x + dx) & 3
            at = t, far, to_x
            arrived(core_in.at[*at], part_recv.at[*at])
            chip_sum[*at] = (own_part[*at] + core_in[*at]).astype(BF16)
            for i in range(2):
                to_y = (zh ^ far) + 2 * i
                slot = 4 * dx + ((to_y - y) & 3)
                start(
                    chip_sum.at[*at, i], plane_in.at[t, slot],
                    plane_send.at[t, far, 2 * dx + i], plane_recv.at[t, slot],
                    device(x=to_x, y=to_y), when=None if dx else to_y != y,
                )

    def line_start(t):
        mine = (t, half ^ zh, x, part)
        total = own_part[mine] + core_in[mine]
        for p in range(1, 16):
            arrived(plane_in.at[t, p], plane_recv.at[t, p])
        for p in range(1, 16):
            total = total + plane_in[t, p].astype(F32)
        for k in range(4):
            r, col = 8 * (k >> 1), 384 * (k & 1)
            quarter[t, k] = total[r : r + 8, col : col + 384]
        for d in (2, 1, 3):
            to_b = (b + d) & 3
            start(
                quarter.at[t, to_b ^ (a & 2)], line_in.at[t, d - 1],
                line_send.at[t, d - 1], line_recv.at[t, d - 1], device(z=a * 4 + to_b),
            )

    def far_start(t):
        total = quarter[t, piece]
        for d in range(1, 4):
            arrived(line_in.at[t, d - 1], line_recv.at[t, d - 1])
            total = total + line_in[t, d - 1]
        line_sum[t] = total
        for d in (2, 1, 3):
            start(
                line_sum.at[t], far_in.at[t, d - 1], far_send.at[t, d - 1], far_recv.at[t, d - 1],
                device(z=far_z(d)), when=(((a + d) & 3) >> 1) == (y & 1),
            )

    def all_start(t):
        @pl.when(holder)
        def _():
            total = line_sum[t]
            for d in range(1, 4):
                arrived(far_in.at[t, d - 1], far_recv.at[t, d - 1])
                total = total + far_in[t, d - 1]
            result[t, part, piece] = total

        for q in range(15, 0, -1):
            start(
                result.at[t, part, piece], result.at[t, part, piece],
                all_send.at[t, q - 1], all_recv.at[t, part, piece],
                device(y=(y + (q >> 2)) & 3, z=a * 4 + ((b + (q & 3)) & 3)), when=holder,
            )

    def finish(t):
        for i in range(2):
            for k in range(4):
                mine = holder & (i == part) & (k == piece)

                @pl.when(jnp.logical_not(mine))
                def _():
                    arrived(result.at[t, i, k], all_recv.at[t, i, k])

                r, col = 16 * i + 8 * (k >> 1), 384 * (k & 1)
                fg_out[t, r : r + 8, col : col + 384] = result[t, i, k]

    send_edge(0)
    send_x(0)
    send_edge(1)
    send_x(1)
    load_w.wait()
    load_m.wait()
    low[0] = w[...].astype(BF16)
    pass_near(0)
    have_edge(0)
    send_token()
    have_core(0, 0)
    block_errors(0, 0)
    pass_near(1)
    have_edge(1)
    products(0, 0)
    plane_start(0, 0)
    pass_far(0)
    pass_token()
    have_core(0, 1)
    block_errors(0, 1)
    update(0)
    products(0, 1)
    pass_far(1)
    have_core(1, 0)
    block_errors(1, 0)
    plane_start(0, 1)
    products(1, 0)
    have_core(1, 1)
    block_errors(1, 1)
    plane_start(1, 0)
    products(1, 1)
    plane_start(1, 1)
    line_start(0)
    have_token()
    far_start(0)
    line_start(1)
    update(1)
    far_start(1)
    all_start(0)
    all_start(1)
    finish(0)
    finish(1)
    for done, when in pending:
        if when is None:
            done()
        else:
            pl.when(when)(done)


def store(w, m, fg, w_out, m_out, fg_out, sems):
    copies = [pltpu.make_async_copy(fg, fg_out, sems.at[0])]
    for src, dst in ((w, w_out), (m, m_out)):
        for i in range(4):
            at = pl.ds(i * (LAB // 4), LAB // 4)
            copies.append(pltpu.make_async_copy(src.at[at], dst.at[at], sems.at[len(copies)]))
    for copy in copies:
        copy.start()
    for copy in copies:
        copy.wait()


def per_device(pool_features, pool_labels, pool_counts, batch_rows, weights, momentum):
    vmem, hbm = pl.BlockSpec(memory_space=pltpu.VMEM), pl.BlockSpec(memory_space=pltpu.HBM)
    dma = pltpu.SemaphoreType.DMA
    part = (2, 2, NX, 2, 16, WIDTH)
    shapes = (
        jax.ShapeDtypeStruct(weights.shape, F32),
        jax.ShapeDtypeStruct(momentum.shape, F32),
        jax.ShapeDtypeStruct((2, GRP, WIDTH), F32),
    )
    results = pl.pallas_call(
        kernel,
        out_shape=tuple(pltpu.VMEM(s.shape, s.dtype) for s in shapes),
        in_specs=[hbm] * 6,
        out_specs=(vmem, vmem, vmem),
        scratch_shapes=[
            pltpu.VMEM((128, WIDTH), BF16),
            pltpu.VMEM((16, 128), jnp.int32),
            pltpu.VMEM((1, 128), jnp.int32),
            pltpu.VMEM((2, GRP), jnp.int32),
            pltpu.VMEM((2, 2, NX, 2, 16, FULL), BF16),
            pltpu.VMEM((2, 2, NX, 2, 16, WIDTH), BF16),
            pltpu.VMEM((2, LAB, WIDTH), BF16),
            pltpu.VMEM((LAB, 8 * GRP), F32),
            pltpu.VMEM((2, 2, LAB, 8 * GRP), BF16),
            pltpu.VMEM((LAB, WIDTH), F32),
            pltpu.VMEM(part, F32),
            pltpu.VMEM(part, F32),
            pltpu.VMEM(part, F32),
            pltpu.VMEM(part, BF16),
            pltpu.VMEM((2, 16, 16, WIDTH), BF16),
            pltpu.VMEM((2, 4, 8, 384), F32),
            pltpu.VMEM((2, 3, 8, 384), F32),
            pltpu.VMEM((2, 8, 384), F32),
            pltpu.VMEM((2, 3, 8, 384), F32),
            pltpu.VMEM((2, 2, 4, 8, 384), F32),
            dma((2, 3)), dma((2, 3)),
            dma((2, 4)), dma((2,)),
            dma((2, 7)), dma((2, 7)),
            dma((2, 2, NX, 2)), dma((2, 2, NX, 2)),
            dma((2, 2, NX)), dma((2, 2, NX)),
            dma((2, 2, 8)), dma((2, 16)),
            dma((2, 3)), dma((2, 3)),
            dma((2, 3)), dma((2, 3)),
            dma((2, 15)), dma((2, 2, 4)),
            dma((6,)),
            pltpu.SemaphoreType.REGULAR((2,)),
        ],
        compiler_params=pltpu.CompilerParams(
            collective_id=0, has_side_effects=True, vmem_limit_bytes=48 << 20
        ),
    )(
        *(
            pltpu.with_memory_space_constraint(array, pltpu.HBM)
            for array in (
                pool_features, pool_labels.T, pool_counts.reshape(1, -1), batch_rows,
                weights, momentum,
            )
        )
    )
    return pl.pallas_call(
        store,
        out_shape=shapes,
        in_specs=[vmem] * 3,
        out_specs=(hbm,) * 3,
        scratch_shapes=[dma((9,))],
    )(*(pltpu.with_memory_space_constraint(array, pltpu.VMEM) for array in results))


def solution(mesh):
    in_specs = (
        P("rows", None),
        P("rows", None),
        P("rows"),
        P(None, "rows"),
        P(("rows", "labels"), None),
        P(("rows", "labels"), None),
    )
    out_specs = (P(("rows", "labels"), None), P(("rows", "labels"), None), P(None, "rows", None))
    return jax.shard_map(
        per_device, mesh=mesh, in_specs=in_specs, out_specs=out_specs, check_vma=False
    )
```

```python
import jax
import jax.numpy as jnp
from jax import lax
from jax.experimental import pallas as pl
from jax.experimental.pallas import tpu as pltpu
from jax.sharding import PartitionSpec as P

learn_rate = 0.001
decay_rate = 0.9
MESH = pl.DeviceIdType.MESH
F32, BF16 = jnp.float32, jnp.bfloat16

NX, NY, WIDTH, TAIL, LAB, GRP = 4, 4, 768, 128, 384, 32
FULL = WIDTH + TAIL
COUNT_LANE = 48


def one_hot(cond):
    return jnp.where(cond, 1.0, 0.0).astype(BF16)


def iota(shape, dim):
    return lax.broadcasted_iota(jnp.int32, shape, dim)


def dot(a, b, dims):
    return lax.dot_general(a, b, (dims, ((), ())), preferred_element_type=F32)


def kernel(
    pool_in, labels_in, counts_in, rows_in, w_in, m_in,
    w, m, fg_out,
    pool, labels, counts, batch_rows, feats0, feats1, low, logits, errs, grads, own_part, other_part, core_in, chip_sum,
    plane_in, quarter, line_in, line_sum, far_in, result,
    x_send, x_recv, edge_send, edge_recv, pair_send, pair_recv, core_send, core_recv, part_send, part_recv,
    plane_send, plane_recv, line_send, line_recv, far_send, far_recv, all_send, all_recv, local, token,
):
    rows_at, labels_at = lax.axis_index("rows"), lax.axis_index("labels")
    zh, x, c = rows_at >> 3, (rows_at >> 1) & 3, rows_at & 1
    y, zl = labels_at >> 3, labels_at & 7
    z = zh * 8 + zl
    a, b = z >> 2, z & 3
    edge = (zl == 0) | (zl == 7)
    inner = (zl == 3) | (zl == 4)
    next_line = zh * 8 + 7 - zl
    holder = zh == (y & 1)
    half, part = y & 1, y >> 1
    piece = b ^ (a & 2)
    pending = []
    feats = (feats0, feats1)

    def far_z(d):
        to = (a + d) & 3
        return to * 4 + (piece ^ (to & 2))

    def device(x=x, y=y, z=z, c=c):
        z = z & 15
        return ((z >> 3) * 8 + x * 2 + c, y * 8 + (z & 7))

    def remote(src, dst, send, recv, to):
        return pltpu.make_async_remote_copy(
            src_ref=src, dst_ref=dst, send_sem=send, recv_sem=recv,
            device_id=to, device_id_type=MESH,
        )

    def start(*args, when=None):
        def go():
            remote(*args).start()

        def done():
            remote(*args).wait_send()

        pending.append((done, when))
        if when is None:
            go()
        else:
            pl.when(when)(go)

    def arrived(dst, recv):
        remote(dst, dst, recv, recv, device(c=1 - c)).wait_recv()

    load_w = pltpu.make_async_copy(w_in, w, local.at[0])
    load_m = pltpu.make_async_copy(m_in, m, local.at[1])
    small = [
        pltpu.make_async_copy(src, dst, local.at[2 + i])
        for i, (src, dst) in enumerate(
            ((pool_in, pool), (labels_in, labels), (counts_in, counts), (rows_in, batch_rows))
        )
    ]
    for copy in small:
        copy.start()
    load_w.start()
    load_m.start()

    barrier = pltpu.get_barrier_semaphore()

    def greet(to):
        pl.semaphore_signal(barrier, inc=1, device_id=to, device_id_type=MESH)

    for d in (2, 1, 3):
        greet(device(z=a * 4 + ((b + d) & 3)))
    for d in (2, 1, 3):
        greet(device(x=(x + d) & 3))
        greet(device(y=(y + d) & 3))
    source_z = jnp.where(zl < 4, zh * 8 + 15, zh * 8 + 8)
    greet(device(z=source_z))
    greet(device(c=1 - c))

    @pl.when(inner)
    def _():
        greet(device(z=next_line))

    for copy in small:
        copy.wait()
    lists = labels[...]
    tail = jnp.zeros((128, TAIL), F32)
    for d in range(3):
        digit = ((lists >> (6 * d)) & 63).astype(F32).astype(BF16)
        lane = iota((16, TAIL), 1) & 63
        place = one_hot(iota((16, TAIL), 0) + 16 * d == lane)
        tail = tail + dot(digit, place, ((0,), (0,)))
    on_diagonal = iota((128, 128), 0) == iota((128, 128), 1)
    diagonal = jnp.where(on_diagonal, counts[...].astype(F32), 0.0).astype(BF16)
    at_count = one_hot((iota((128, TAIL), 1) & 63) == COUNT_LANE)
    tail = (tail + dot(diagonal, at_count, ((1,), (0,)))).astype(BF16)
    chosen = [
        one_hot(iota((128, GRP), 0) == batch_rows[pl.ds(t, 1), :]) for t in range(2)
    ]
    for t in range(2):
        features = dot(chosen[t], pool[...], ((0,), (0,))).astype(BF16)
        feats[t][0, 0, x, :, :, :WIDTH] = features.reshape(2, 16, WIDTH)
    lists = [dot(chosen[t], tail, ((0,), (0,))) for t in range(2)]
    lists = jnp.where(iota((GRP, TAIL), 1) < 64, lists[0], lists[1]).astype(BF16)
    feats0[0, 0, x, :, :, WIDTH:] = lists.reshape(2, 16, TAIL)

    pl.semaphore_wait(
        barrier, 10 + jnp.where(edge, 4, 0) + jnp.where(inner, 1, 0)
    )

    def send_edge(t):
        for k in (3, 2, 1, 0):
            to_z = jnp.where(zl == 0, z - 1 - k, z + 1 + k)
            start(
                feats[t].at[0, 0, x, half], feats[t].at[1, 0, x, half],
                edge_send.at[t, k], edge_recv.at[t], device(z=to_z), when=edge,
            )

    def send_core(*at):
        start(
            feats[at[0]].at[at[1], 0, *at[2:]], feats[at[0]].at[at[1], 1, *at[2:]],
            core_send.at[*at, *[0] * (4 - len(at))], core_recv.at[*at, *[0] * (4 - len(at))],
            device(c=1 - c),
        )

    def send_x(t):
        for d in (2, 1, 3):
            start(
                feats[t].at[0, 0, x], feats[t].at[0, 0, x],
                x_send.at[t, d - 1], x_recv.at[t, d - 1], device(x=(x + d) & 3),
            )
        send_core(t, 0, x)

    def pass_near(t):
        for d in (1, 3, 2):
            at = (x - d) & 3
            arrived(feats[t].at[0, 0, at], x_recv.at[t, d - 1])
            send_core(t, 0, at)

    def have_edge(t):
        arrived(feats[t].at[1, 0, x, half], edge_recv.at[t])
        for q in (5, 4, 3, 7, 2, 6, 1):
            start(
                feats[t].at[1, 0, x, half], feats[t].at[1, 0, x, half],
                pair_send.at[t, q - 1], pair_recv.at[t, q - 1],
                device(x=(x + (q >> 1)) & 3, y=y ^ (q & 1)),
            )
        send_core(t, 1, x, half)

    def pass_far(t):
        for q in (1, 2, 6, 3, 7, 4, 5):
            at = (x - (q >> 1)) & 3, half ^ (q & 1)
            arrived(feats[t].at[1, 0, *at], pair_recv.at[t, q - 1])
            send_core(t, 1, *at)

    def send_token():
        @pl.when(inner)
        def _():
            pl.semaphore_signal(
                token.at[0], inc=1, device_id=device(z=next_line), device_id_type=MESH
            )

    def pass_token():
        @pl.when(inner)
        def _():
            pl.semaphore_wait(token.at[0], 1)
            for d in (2, 1, 3):
                pl.semaphore_signal(
                    token.at[1], inc=1, device_id=device(z=a * 4 + ((b + d) & 3)),
                    device_id_type=MESH,
                )

    def have_token():
        @pl.when(jnp.logical_not(inner))
        def _():
            pl.semaphore_wait(token.at[1], 1)

    def have_core(t, far):
        for at in range(NX):
            if far:
                for i in range(2):
                    arrived(feats[t].at[1, 1, at, i], core_recv.at[t, 1, at, i])
            else:
                arrived(feats[t].at[0, 1, at], core_recv.at[t, 0, at, 0])

    base = ((rows_at * 32 + labels_at) * LAB).astype(F32)

    def block_errors(t, far):
        features = feats[t][far, :, :, :, :, :WIDTH].reshape(8 * GRP, WIDTH)
        lists = feats0[far, :, :, :, :, WIDTH:].reshape(8 * GRP, TAIL)
        logits[...] = dot(low[t], features, ((1,), (1,)))
        slot, lane = iota((16, TAIL), 0), iota((16, TAIL), 1) - 64 * t
        weight = jnp.zeros((16, TAIL), F32)
        for d in range(3):
            weight = jnp.where(lane == slot + 16 * d, float(64**d), weight)
        ids = dot(weight.astype(BF16), lists, ((1,), (1,)))
        used = dot(one_hot(lane == COUNT_LANE), lists, ((1,), (1,)))
        in_list = iota(ids.shape, 0).astype(F32) < used
        ids = jnp.where(in_list, ids - base, -1.0)

        def chunk(i, _):
            at = pl.ds(pl.multiple_of(i * 64, 64), 64)
            label = (iota((64, 8 * GRP), 0) + i * 64).astype(F32)
            hit = ids[0:1, :] == label
            for k in range(1, 16):
                hit = hit | (ids[k : k + 1, :] == label)
            targets = jnp.where(hit, 1.0, 0.0)
            errs[t, far, at, :] = (jax.nn.sigmoid(logits[at, :]) - targets).astype(BF16)
            return 0

        lax.fori_loop(0, LAB // 64, chunk, 0)
        part = dot(errs[t, far], features, ((1,), (0,)))
        if far:
            grads[...] += part
        else:
            grads[...] = part

    def update(t):
        def chunk(i, _):
            at = pl.ds(pl.multiple_of(i * 64, 64), 64)
            moment = decay_rate * m[at, :] + grads[at, :]
            weight = w[at, :] - learn_rate * moment
            m[at, :] = moment
            w[at, :] = weight
            if t == 0:
                low[1, at, :] = weight.astype(BF16)
            return 0

        lax.fori_loop(0, LAB // 64, chunk, 0)

    def products(t, far):
        for other in (1, 0):
            cols = pl.ds(other * 128, 128)
            product = dot(errs[t, far, :, cols], low[t], ((0,), (0,)))
            product = product.reshape(NX, 2, 16, WIDTH)
            if other:
                other_part[t, far] = product
                for d in (1, 3, 2, 0):
                    at = t, far, (x + d) & 3
                    start(
                        other_part.at[*at], core_in.at[*at],
                        part_send.at[*at], part_recv.at[*at], device(c=1 - c),
                    )
            else:
                own_part[t, far] = product

    def plane_start(t, far):
        for dx in (1, 3, 2, 0):
            to_x = (x + dx) & 3
            at = t, far, to_x
            arrived(core_in.at[*at], part_recv.at[*at])
            chip_sum[*at] = (own_part[*at] + core_in[*at]).astype(BF16)
            for i in range(2):
                to_y = (zh ^ far) + 2 * i
                slot = 4 * dx + ((to_y - y) & 3)
                start(
                    chip_sum.at[*at, i], plane_in.at[t, slot],
                    plane_send.at[t, far, 2 * dx + i], plane_recv.at[t, slot],
                    device(x=to_x, y=to_y), when=None if dx else to_y != y,
                )

    def line_start(t):
        mine = (t, half ^ zh, x, part)
        total = own_part[mine] + core_in[mine]
        for p in range(1, 16):
            arrived(plane_in.at[t, p], plane_recv.at[t, p])
        for p in range(1, 16):
            total = total + plane_in[t, p].astype(F32)
        for k in range(4):
            r, col = 8 * (k >> 1), 384 * (k & 1)
            quarter[t, k] = total[r : r + 8, col : col + 384]
        for d in (2, 1, 3):
            to_b = (b + d) & 3
            start(
                quarter.at[t, to_b ^ (a & 2)], line_in.at[t, d - 1],
                line_send.at[t, d - 1], line_recv.at[t, d - 1], device(z=a * 4 + to_b),
            )

    def far_start(t):
        total = quarter[t, piece]
        for d in range(1, 4):
            arrived(line_in.at[t, d - 1], line_recv.at[t, d - 1])
            total = total + line_in[t, d - 1]
        line_sum[t] = total
        for d in (2, 1, 3):
            start(
                line_sum.at[t], far_in.at[t, d - 1], far_send.at[t, d - 1], far_recv.at[t, d - 1],
                device(z=far_z(d)), when=(((a + d) & 3) >> 1) == (y & 1),
            )

    def all_start(t):
        @pl.when(holder)
        def _():
            total = line_sum[t]
            for d in range(1, 4):
                arrived(far_in.at[t, d - 1], far_recv.at[t, d - 1])
                total = total + far_in[t, d - 1]
            result[t, part, piece] = total

        def hops(q):
            return 2 - abs((q >> 2) - 2) + 2 * ((q & 3) > 0)

        for q in sorted(range(1, 16), key=hops, reverse=True):
            start(
                result.at[t, part, piece], result.at[t, part, piece],
                all_send.at[t, q - 1], all_recv.at[t, part, piece],
                device(y=(y + (q >> 2)) & 3, z=a * 4 + ((b + (q & 3)) & 3)), when=holder,
            )

    def finish(t):
        for i in range(2):
            for k in range(4):
                mine = holder & (i == part) & (k == piece)

                @pl.when(jnp.logical_not(mine))
                def _():
                    arrived(result.at[t, i, k], all_recv.at[t, i, k])

                r, col = 16 * i + 8 * (k >> 1), 384 * (k & 1)
                fg_out[t, r : r + 8, col : col + 384] = result[t, i, k]

    send_edge(0)
    send_x(0)
    send_edge(1)
    send_x(1)
    load_w.wait()
    load_m.wait()
    low[0] = w[...].astype(BF16)
    pass_near(0)
    have_edge(0)
    send_token()
    have_core(0, 0)
    block_errors(0, 0)
    pass_near(1)
    have_edge(1)
    products(0, 0)
    plane_start(0, 0)
    pass_far(0)
    pass_token()
    have_core(0, 1)
    block_errors(0, 1)
    update(0)
    products(0, 1)
    pass_far(1)
    have_core(1, 0)
    block_errors(1, 0)
    plane_start(0, 1)
    products(1, 0)
    have_core(1, 1)
    block_errors(1, 1)
    plane_start(1, 0)
    products(1, 1)
    plane_start(1, 1)
    line_start(0)
    have_token()
    far_start(0)
    line_start(1)
    update(1)
    far_start(1)
    all_start(0)
    all_start(1)
    finish(0)
    finish(1)
    for done, when in pending:
        if when is None:
            done()
        else:
            pl.when(when)(done)


def store(w, m, fg, w_out, m_out, fg_out, sems):
    copies = [pltpu.make_async_copy(fg, fg_out, sems.at[0])]
    for src, dst in ((w, w_out), (m, m_out)):
        for i in range(4):
            at = pl.ds(i * (LAB // 4), LAB // 4)
            copies.append(pltpu.make_async_copy(src.at[at], dst.at[at], sems.at[len(copies)]))
    for copy in copies:
        copy.start()
    for copy in copies:
        copy.wait()


def per_device(pool_features, pool_labels, pool_counts, batch_rows, weights, momentum):
    vmem, hbm = pl.BlockSpec(memory_space=pltpu.VMEM), pl.BlockSpec(memory_space=pltpu.HBM)
    dma = pltpu.SemaphoreType.DMA
    part = (2, 2, NX, 2, 16, WIDTH)
    shapes = (
        jax.ShapeDtypeStruct(weights.shape, F32),
        jax.ShapeDtypeStruct(momentum.shape, F32),
        jax.ShapeDtypeStruct((2, GRP, WIDTH), F32),
    )
    results = pl.pallas_call(
        kernel,
        out_shape=tuple(pltpu.VMEM(s.shape, s.dtype) for s in shapes),
        in_specs=[hbm] * 6,
        out_specs=(vmem, vmem, vmem),
        scratch_shapes=[
            pltpu.VMEM((128, WIDTH), BF16),
            pltpu.VMEM((16, 128), jnp.int32),
            pltpu.VMEM((1, 128), jnp.int32),
            pltpu.VMEM((2, GRP), jnp.int32),
            pltpu.VMEM((2, 2, NX, 2, 16, FULL), BF16),
            pltpu.VMEM((2, 2, NX, 2, 16, WIDTH), BF16),
            pltpu.VMEM((2, LAB, WIDTH), BF16),
            pltpu.VMEM((LAB, 8 * GRP), F32),
            pltpu.VMEM((2, 2, LAB, 8 * GRP), BF16),
            pltpu.VMEM((LAB, WIDTH), F32),
            pltpu.VMEM(part, F32),
            pltpu.VMEM(part, F32),
            pltpu.VMEM(part, F32),
            pltpu.VMEM(part, BF16),
            pltpu.VMEM((2, 16, 16, WIDTH), BF16),
            pltpu.VMEM((2, 4, 8, 384), F32),
            pltpu.VMEM((2, 3, 8, 384), F32),
            pltpu.VMEM((2, 8, 384), F32),
            pltpu.VMEM((2, 3, 8, 384), F32),
            pltpu.VMEM((2, 2, 4, 8, 384), F32),
            dma((2, 3)), dma((2, 3)),
            dma((2, 4)), dma((2,)),
            dma((2, 7)), dma((2, 7)),
            dma((2, 2, NX, 2)), dma((2, 2, NX, 2)),
            dma((2, 2, NX)), dma((2, 2, NX)),
            dma((2, 2, 8)), dma((2, 16)),
            dma((2, 3)), dma((2, 3)),
            dma((2, 3)), dma((2, 3)),
            dma((2, 15)), dma((2, 2, 4)),
            dma((6,)),
            pltpu.SemaphoreType.REGULAR((2,)),
        ],
        compiler_params=pltpu.CompilerParams(
            collective_id=0, has_side_effects=True, vmem_limit_bytes=48 << 20
        ),
    )(
        *(
            pltpu.with_memory_space_constraint(array, pltpu.HBM)
            for array in (
                pool_features, pool_labels.T, pool_counts.reshape(1, -1), batch_rows,
                weights, momentum,
            )
        )
    )
    return pl.pallas_call(
        store,
        out_shape=shapes,
        in_specs=[vmem] * 3,
        out_specs=(hbm,) * 3,
        scratch_shapes=[dma((9,))],
    )(*(pltpu.with_memory_space_constraint(array, pltpu.VMEM) for array in results))


def solution(mesh):
    in_specs = (
        P("rows", None),
        P("rows", None),
        P("rows"),
        P(None, "rows"),
        P(("rows", "labels"), None),
        P(("rows", "labels"), None),
    )
    out_specs = (P(("rows", "labels"), None), P(("rows", "labels"), None), P(None, "rows", None))
    return jax.shard_map(
        per_device, mesh=mesh, in_specs=in_specs, out_specs=out_specs, check_vma=False
    )
```

```python
import jax
import jax.numpy as jnp
from jax import lax
from jax.experimental import pallas as pl
from jax.experimental.pallas import tpu as pltpu
from jax.sharding import PartitionSpec as P

learn_rate = 0.001
decay_rate = 0.9
MESH = pl.DeviceIdType.MESH
F32, BF16 = jnp.float32, jnp.bfloat16

NX, NY, WIDTH, TAIL, LAB, GRP = 4, 4, 768, 128, 384, 32
FULL = WIDTH + TAIL
COUNT_LANE = 48


def one_hot(cond):
    return jnp.where(cond, 1.0, 0.0).astype(BF16)


def iota(shape, dim):
    return lax.broadcasted_iota(jnp.int32, shape, dim)


def dot(a, b, dims):
    return lax.dot_general(a, b, (dims, ((), ())), preferred_element_type=F32)


def kernel(
    pool_in, labels_in, counts_in, rows_in, w_in, m_in,
    w, m, fg_out,
    pool, labels, counts, batch_rows, feats0, feats1, low, logits, errs, grads, own_part, other_part, core_in, chip_sum,
    plane_in, quarter, line_in, line_sum, far_in, result,
    x_send, x_recv, edge_send, edge_recv, pair_send, pair_recv, core_send, core_recv, part_send, part_recv,
    plane_send, plane_recv, line_send, line_recv, far_send, far_recv, all_send, all_recv, local, token,
):
    rows_at, labels_at = lax.axis_index("rows"), lax.axis_index("labels")
    zh, x, c = rows_at >> 3, (rows_at >> 1) & 3, rows_at & 1
    y, zl = labels_at >> 3, labels_at & 7
    z = zh * 8 + zl
    a, b = z >> 2, z & 3
    edge = (zl == 0) | (zl == 7)
    inner = (zl == 3) | (zl == 4)
    next_line = zh * 8 + 7 - zl
    holder = zh == (y & 1)
    half, part = y & 1, y >> 1
    piece = b ^ (a & 2)
    pending = []
    feats = (feats0, feats1)

    def far_z(d):
        to = (a + d) & 3
        return to * 4 + (piece ^ (to & 2))

    def device(x=x, y=y, z=z, c=c):
        z = z & 15
        return ((z >> 3) * 8 + x * 2 + c, y * 8 + (z & 7))

    def remote(src, dst, send, recv, to):
        return pltpu.make_async_remote_copy(
            src_ref=src, dst_ref=dst, send_sem=send, recv_sem=recv,
            device_id=to, device_id_type=MESH,
        )

    def start(*args, when=None):
        def go():
            remote(*args).start()

        def done():
            remote(*args).wait_send()

        pending.append((done, when))
        if when is None:
            go()
        else:
            pl.when(when)(go)

    def arrived(dst, recv):
        remote(dst, dst, recv, recv, device(c=1 - c)).wait_recv()

    load_w = pltpu.make_async_copy(w_in, w, local.at[0])
    load_m = pltpu.make_async_copy(m_in, m, local.at[1])
    small = [
        pltpu.make_async_copy(src, dst, local.at[2 + i])
        for i, (src, dst) in enumerate(
            ((pool_in, pool), (labels_in, labels), (counts_in, counts), (rows_in, batch_rows))
        )
    ]
    for copy in small:
        copy.start()
    load_w.start()
    load_m.start()

    barrier = pltpu.get_barrier_semaphore()

    def greet(to):
        pl.semaphore_signal(barrier, inc=1, device_id=to, device_id_type=MESH)

    for d in (2, 1, 3):
        greet(device(z=a * 4 + ((b + d) & 3)))
    for d in (2, 1, 3):
        greet(device(x=(x + d) & 3))
        greet(device(y=(y + d) & 3))
    source_z = jnp.where(zl < 4, zh * 8 + 15, zh * 8 + 8)
    greet(device(z=source_z))
    greet(device(c=1 - c))

    @pl.when(inner)
    def _():
        greet(device(z=next_line))

    for copy in small:
        copy.wait()
    lists = labels[...]
    tail = jnp.zeros((128, TAIL), F32)
    for d in range(3):
        digit = ((lists >> (6 * d)) & 63).astype(F32).astype(BF16)
        lane = iota((16, TAIL), 1) & 63
        place = one_hot(iota((16, TAIL), 0) + 16 * d == lane)
        tail = tail + dot(digit, place, ((0,), (0,)))
    on_diagonal = iota((128, 128), 0) == iota((128, 128), 1)
    diagonal = jnp.where(on_diagonal, counts[...].astype(F32), 0.0).astype(BF16)
    at_count = one_hot((iota((128, TAIL), 1) & 63) == COUNT_LANE)
    tail = (tail + dot(diagonal, at_count, ((1,), (0,)))).astype(BF16)
    chosen = [
        one_hot(iota((128, GRP), 0) == batch_rows[pl.ds(t, 1), :]) for t in range(2)
    ]
    for t in range(2):
        features = dot(chosen[t], pool[...], ((0,), (0,))).astype(BF16)
        feats[t][0, 0, x, :, :, :WIDTH] = features.reshape(2, 16, WIDTH)
    lists = [dot(chosen[t], tail, ((0,), (0,))) for t in range(2)]
    lists = jnp.where(iota((GRP, TAIL), 1) < 64, lists[0], lists[1]).astype(BF16)
    feats0[0, 0, x, :, :, WIDTH:] = lists.reshape(2, 16, TAIL)

    pl.semaphore_wait(
        barrier, 10 + jnp.where(edge, 4, 0) + jnp.where(inner, 1, 0)
    )

    def send_edge(t):
        for k in (3, 2, 1, 0):
            to_z = jnp.where(zl == 0, z - 1 - k, z + 1 + k)
            start(
                feats[t].at[0, 0, x, half], feats[t].at[1, 0, x, half],
                edge_send.at[t, k], edge_recv.at[t], device(z=to_z), when=edge,
            )

    def send_core(*at):
        start(
            feats[at[0]].at[at[1], 0, *at[2:]], feats[at[0]].at[at[1], 1, *at[2:]],
            core_send.at[*at, *[0] * (4 - len(at))], core_recv.at[*at, *[0] * (4 - len(at))],
            device(c=1 - c),
        )

    def send_x(t):
        for d in (2, 1, 3):
            start(
                feats[t].at[0, 0, x], feats[t].at[0, 0, x],
                x_send.at[t, d - 1], x_recv.at[t, d - 1], device(x=(x + d) & 3),
            )
        send_core(t, 0, x)

    def pass_near(t):
        for d in (1, 3, 2):
            at = (x - d) & 3
            arrived(feats[t].at[0, 0, at], x_recv.at[t, d - 1])
            send_core(t, 0, at)

    def have_edge(t):
        arrived(feats[t].at[1, 0, x, half], edge_recv.at[t])
        for q in (5, 4, 3, 7, 2, 6, 1):
            start(
                feats[t].at[1, 0, x, half], feats[t].at[1, 0, x, half],
                pair_send.at[t, q - 1], pair_recv.at[t, q - 1],
                device(x=(x + (q >> 1)) & 3, y=y ^ (q & 1)),
            )
        send_core(t, 1, x, half)

    def pass_far(t):
        for q in (1, 2, 6, 3, 7, 4, 5):
            at = (x - (q >> 1)) & 3, half ^ (q & 1)
            arrived(feats[t].at[1, 0, *at], pair_recv.at[t, q - 1])
            send_core(t, 1, *at)

    def send_token():
        @pl.when(inner)
        def _():
            pl.semaphore_signal(
                token.at[0], inc=1, device_id=device(z=next_line), device_id_type=MESH
            )

    def pass_token():
        @pl.when(inner)
        def _():
            pl.semaphore_wait(token.at[0], 1)
            for d in (2, 1, 3):
                pl.semaphore_signal(
                    token.at[1], inc=1, device_id=device(z=a * 4 + ((b + d) & 3)),
                    device_id_type=MESH,
                )

    def have_token():
        @pl.when(jnp.logical_not(inner))
        def _():
            pl.semaphore_wait(token.at[1], 1)

    def have_core(t, far):
        for at in range(NX):
            if far:
                for i in range(2):
                    arrived(feats[t].at[1, 1, at, i], core_recv.at[t, 1, at, i])
            else:
                arrived(feats[t].at[0, 1, at], core_recv.at[t, 0, at, 0])

    base = ((rows_at * 32 + labels_at) * LAB).astype(F32)

    def block_errors(t, far):
        features = feats[t][far, :, :, :, :, :WIDTH].reshape(8 * GRP, WIDTH)
        lists = feats0[far, :, :, :, :, WIDTH:].reshape(8 * GRP, TAIL)
        logits[...] = dot(low[t], features, ((1,), (1,)))
        slot, lane = iota((16, TAIL), 0), iota((16, TAIL), 1) - 64 * t
        weight = jnp.zeros((16, TAIL), F32)
        for d in range(3):
            weight = jnp.where(lane == slot + 16 * d, float(64**d), weight)
        ids = dot(weight.astype(BF16), lists, ((1,), (1,)))
        used = dot(one_hot(lane == COUNT_LANE), lists, ((1,), (1,)))
        in_list = iota(ids.shape, 0).astype(F32) < used
        ids = jnp.where(in_list, ids - base, -1.0)

        def chunk(i, _):
            at = pl.ds(pl.multiple_of(i * 64, 64), 64)
            label = (iota((64, 8 * GRP), 0) + i * 64).astype(F32)
            hit = ids[0:1, :] == label
            for k in range(1, 16):
                hit = hit | (ids[k : k + 1, :] == label)
            targets = jnp.where(hit, 1.0, 0.0)
            errs[t, far, at, :] = (jax.nn.sigmoid(logits[at, :]) - targets).astype(BF16)
            return 0

        lax.fori_loop(0, LAB // 64, chunk, 0)
        part = dot(errs[t, far], features, ((1,), (0,)))
        if far:
            grads[...] += part
        else:
            grads[...] = part

    def update(t):
        def chunk(i, _):
            at = pl.ds(pl.multiple_of(i * 64, 64), 64)
            moment = decay_rate * m[at, :] + grads[at, :]
            weight = w[at, :] - learn_rate * moment
            m[at, :] = moment
            w[at, :] = weight
            if t == 0:
                low[1, at, :] = weight.astype(BF16)
            return 0

        lax.fori_loop(0, LAB // 64, chunk, 0)

    def products(t, far):
        for other in (1, 0):
            cols = pl.ds(other * 128, 128)
            product = dot(errs[t, far, :, cols], low[t], ((0,), (0,)))
            product = product.reshape(NX, 2, 16, WIDTH)
            if other:
                other_part[t, far] = product
                for d in (1, 3, 2, 0):
                    at = t, far, (x + d) & 3
                    start(
                        other_part.at[*at], core_in.at[*at],
                        part_send.at[*at], part_recv.at[*at], device(c=1 - c),
                    )
            else:
                own_part[t, far] = product

    def plane_start(t, far):
        for dx in (1, 3, 2, 0):
            to_x = (x + dx) & 3
            at = t, far, to_x
            arrived(core_in.at[*at], part_recv.at[*at])
            chip_sum[*at] = (own_part[*at] + core_in[*at]).astype(BF16)
            for i in range(2):
                to_y = (zh ^ far) + 2 * i
                slot = 4 * dx + ((to_y - y) & 3)
                start(
                    chip_sum.at[*at, i], plane_in.at[t, slot],
                    plane_send.at[t, far, 2 * dx + i], plane_recv.at[t, slot],
                    device(x=to_x, y=to_y), when=None if dx else to_y != y,
                )

    def line_start(t):
        mine = (t, half ^ zh, x, part)
        total = own_part[mine] + core_in[mine]
        for p in range(1, 16):
            arrived(plane_in.at[t, p], plane_recv.at[t, p])
        for p in range(1, 16):
            total = total + plane_in[t, p].astype(F32)
        for k in range(4):
            r, col = 8 * (k >> 1), 384 * (k & 1)
            quarter[t, k] = total[r : r + 8, col : col + 384]
        for d in (2, 1, 3):
            to_b = (b + d) & 3
            start(
                quarter.at[t, to_b ^ (a & 2)], line_in.at[t, d - 1],
                line_send.at[t, d - 1], line_recv.at[t, d - 1], device(z=a * 4 + to_b),
            )

    def far_start(t):
        total = quarter[t, piece]
        for d in range(1, 4):
            arrived(line_in.at[t, d - 1], line_recv.at[t, d - 1])
            total = total + line_in[t, d - 1]
        line_sum[t] = total
        for d in (2, 1, 3):
            start(
                line_sum.at[t], far_in.at[t, d - 1], far_send.at[t, d - 1], far_recv.at[t, d - 1],
                device(z=far_z(d)), when=(((a + d) & 3) >> 1) == (y & 1),
            )

    def all_start(t):
        @pl.when(holder)
        def _():
            total = line_sum[t]
            for d in range(1, 4):
                arrived(far_in.at[t, d - 1], far_recv.at[t, d - 1])
                total = total + far_in[t, d - 1]
            result[t, part, piece] = total

        def hops(q):
            return 2 - abs((q >> 2) - 2) + 2 * ((q & 3) > 0)

        for q in sorted(range(1, 16), key=hops, reverse=True):
            start(
                result.at[t, part, piece], result.at[t, part, piece],
                all_send.at[t, q - 1], all_recv.at[t, part, piece],
                device(y=(y + (q >> 2)) & 3, z=a * 4 + ((b + (q & 3)) & 3)), when=holder,
            )

    def finish(t):
        for i in range(2):
            for k in range(4):
                mine = holder & (i == part) & (k == piece)

                @pl.when(jnp.logical_not(mine))
                def _():
                    arrived(result.at[t, i, k], all_recv.at[t, i, k])

                r, col = 16 * i + 8 * (k >> 1), 384 * (k & 1)
                fg_out[t, r : r + 8, col : col + 384] = result[t, i, k]

    send_edge(0)
    send_x(0)
    send_edge(1)
    send_x(1)
    load_w.wait()
    load_m.wait()
    low[0] = w[...].astype(BF16)
    pass_near(0)
    have_edge(0)
    send_token()
    have_core(0, 0)
    block_errors(0, 0)
    pass_near(1)
    have_edge(1)
    products(0, 0)
    plane_start(0, 0)
    pass_far(0)
    pass_token()
    have_core(0, 1)
    block_errors(0, 1)
    update(0)
    products(0, 1)
    pass_far(1)
    have_core(1, 0)
    block_errors(1, 0)
    plane_start(0, 1)
    products(1, 0)
    have_core(1, 1)
    block_errors(1, 1)
    plane_start(1, 0)
    products(1, 1)
    plane_start(1, 1)
    update(1)
    line_start(0)
    have_token()
    far_start(0)
    line_start(1)
    far_start(1)
    all_start(0)
    all_start(1)
    finish(0)
    finish(1)
    for done, when in pending:
        if when is None:
            done()
        else:
            pl.when(when)(done)


def store(w, m, fg, w_out, m_out, fg_out, sems):
    copies = [pltpu.make_async_copy(fg, fg_out, sems.at[0])]
    for src, dst in ((w, w_out), (m, m_out)):
        for i in range(4):
            at = pl.ds(i * (LAB // 4), LAB // 4)
            copies.append(pltpu.make_async_copy(src.at[at], dst.at[at], sems.at[len(copies)]))
    for copy in copies:
        copy.start()
    for copy in copies:
        copy.wait()


def per_device(pool_features, pool_labels, pool_counts, batch_rows, weights, momentum):
    vmem, hbm = pl.BlockSpec(memory_space=pltpu.VMEM), pl.BlockSpec(memory_space=pltpu.HBM)
    dma = pltpu.SemaphoreType.DMA
    part = (2, 2, NX, 2, 16, WIDTH)
    shapes = (
        jax.ShapeDtypeStruct(weights.shape, F32),
        jax.ShapeDtypeStruct(momentum.shape, F32),
        jax.ShapeDtypeStruct((2, GRP, WIDTH), F32),
    )
    results = pl.pallas_call(
        kernel,
        out_shape=tuple(pltpu.VMEM(s.shape, s.dtype) for s in shapes),
        in_specs=[hbm] * 6,
        out_specs=(vmem, vmem, vmem),
        scratch_shapes=[
            pltpu.VMEM((128, WIDTH), BF16),
            pltpu.VMEM((16, 128), jnp.int32),
            pltpu.VMEM((1, 128), jnp.int32),
            pltpu.VMEM((2, GRP), jnp.int32),
            pltpu.VMEM((2, 2, NX, 2, 16, FULL), BF16),
            pltpu.VMEM((2, 2, NX, 2, 16, WIDTH), BF16),
            pltpu.VMEM((2, LAB, WIDTH), BF16),
            pltpu.VMEM((LAB, 8 * GRP), F32),
            pltpu.VMEM((2, 2, LAB, 8 * GRP), BF16),
            pltpu.VMEM((LAB, WIDTH), F32),
            pltpu.VMEM(part, F32),
            pltpu.VMEM(part, F32),
            pltpu.VMEM(part, F32),
            pltpu.VMEM(part, BF16),
            pltpu.VMEM((2, 16, 16, WIDTH), BF16),
            pltpu.VMEM((2, 4, 8, 384), F32),
            pltpu.VMEM((2, 3, 8, 384), F32),
            pltpu.VMEM((2, 8, 384), F32),
            pltpu.VMEM((2, 3, 8, 384), F32),
            pltpu.VMEM((2, 2, 4, 8, 384), F32),
            dma((2, 3)), dma((2, 3)),
            dma((2, 4)), dma((2,)),
            dma((2, 7)), dma((2, 7)),
            dma((2, 2, NX, 2)), dma((2, 2, NX, 2)),
            dma((2, 2, NX)), dma((2, 2, NX)),
            dma((2, 2, 8)), dma((2, 16)),
            dma((2, 3)), dma((2, 3)),
            dma((2, 3)), dma((2, 3)),
            dma((2, 15)), dma((2, 2, 4)),
            dma((6,)),
            pltpu.SemaphoreType.REGULAR((2,)),
        ],
        compiler_params=pltpu.CompilerParams(
            collective_id=0, has_side_effects=True, vmem_limit_bytes=48 << 20
        ),
    )(
        *(
            pltpu.with_memory_space_constraint(array, pltpu.HBM)
            for array in (
                pool_features, pool_labels.T, pool_counts.reshape(1, -1), batch_rows,
                weights, momentum,
            )
        )
    )
    return pl.pallas_call(
        store,
        out_shape=shapes,
        in_specs=[vmem] * 3,
        out_specs=(hbm,) * 3,
        scratch_shapes=[dma((9,))],
    )(*(pltpu.with_memory_space_constraint(array, pltpu.VMEM) for array in results))


def solution(mesh):
    in_specs = (
        P("rows", None),
        P("rows", None),
        P("rows"),
        P(None, "rows"),
        P(("rows", "labels"), None),
        P(("rows", "labels"), None),
    )
    out_specs = (P(("rows", "labels"), None), P(("rows", "labels"), None), P(None, "rows", None))
    return jax.shard_map(
        per_device, mesh=mesh, in_specs=in_specs, out_specs=out_specs, check_vma=False
    )
```
